32 devices in a mesh: clips: 2 (over x), gx: 4 (over y, core), gy: 4 (over z).
Axes of the slice: x: 2, y: 2, z: 4, core: 2. Of those that a mesh axis runs over, the one named last changes fastest.
Arguments:
- fields: float32 [12, 32, 32, 512], P('clips', None, 'gx', 'gy'), parts along dimension 0, may hold values from -6 to 6
- material_map: int32 [64, 32, 512], P('clips', 'gx', 'gy'), parts along dimension 0, may hold values from 0 to 3
- material_eps: float32 [4], replicated, may hold values from 1 to 4
- material_loss: float32 [4], replicated, may hold values from 0 to 0.4
- source_shift: int32 [64, 2], P(('gx', 'gy')), may hold values from -8 to 8
- source_mask: int32 [64, 96, 96], P(('gx', 'gy')), may hold values 0 or 1
- source_weight: float32 [64], P(('gx', 'gy')), may hold values from 0.25 to 4
Outputs:
- final_fields: float32 [12, 32, 32, 512], P('clips', None, 'gx', 'gy'), parts along dimension 0
- image: float32 [512, 1024], P(('gx', 'gy'), 'clips'), parts along dimension 1
The draws below stay inside these ranges and needn't reach their ends.
There are 2 independent parts, one for each index of `clips`. The reference program is written for one: setup_inputs(seed, part) draws one part's arguments, and reference() takes and returns one part's arrays. A program takes and returns all parts, laid end to end along the dimension named above; an argument that names none is the same for every part. Nothing has to cross between parts.
All inputs are finite; a program needn't handle non-finite values. No bound on the sum of `source_mask` on one device may be relied on, other than what follows from the above.
Results may differ from the reference program's by a relative error of at most 0.0014.
The reference program's roundings to bfloat16 on the way (of `orders_b`, `masked` and `columns`) count: a program that leaves them out, or rounds other values in their place, can miss the bound.
Values sent between devices are 32-bit elements; how exact they have to be, the bound alone decides.
A program may use at most 64 MiB of HBM per device.

```python
import math
import jax
import jax.numpy as jnp
from jax import lax

NZ = 32
STEPS = 12
MATS = 4
P_SIZE = 96
Q = 96
M = 512
NX = 32
NY = 512
SOURCES = 64


def plant(entries, rng, low, top_value):
    place = [jax.random.randint(jax.random.fold_in(rng, axis), (), 0, length) for axis, length in enumerate(entries.shape)]
    widest = entries.shape.index(max(entries.shape))
    beside = place[:widest] + [(place[widest] + 1) % entries.shape[widest]] + place[widest + 1:]
    return entries.at[tuple(place)].set(low).at[tuple(beside)].set(top_value)


def block_scale(key, shape, pieces, low, top_value):
    gain, own = 1.0, jax.random.fold_in(key, 6)
    for dim, parts in pieces:
        heights = jnp.exp(jax.random.uniform(jax.random.fold_in(own, dim), (parts,), jnp.float32, low / len(pieces), top_value / len(pieces)))
        gain = gain * jnp.repeat(heights, shape[dim] // parts).reshape([-1 if axis == dim else 1 for axis in range(len(shape))])
    return gain


def scatter_about(own_key, shape, deviation, most, pieces=(), kind=jnp.bfloat16):
    result = jax.random.normal(own_key, shape, jnp.float32) * deviation
    if len(pieces) > 0:
        result = block_scale(own_key, shape, pieces, -0.22, 0.18) * result
    return jnp.clip(result, min=-most, max=most).astype(kind)


def setup_inputs(seed: int = 0, part: int = 0) -> dict:
    keys = jax.random.split(jax.random.key(seed), 8)
    part_keys = jax.random.split(jax.random.fold_in(keys[7], part), 8)
    fields = scatter_about(part_keys[0], (6, NZ, NX, NY), 1.0, 6.0, ((2, 4), (3, 4)), jnp.float32)
    material_map = plant(jax.random.randint(part_keys[1], (NZ, NX, NY), 0, MATS), jax.random.fold_in(part_keys[1], 1), 0, MATS - 1).astype(jnp.int32)
    material_eps = jnp.clip(jnp.exp(jax.random.uniform(keys[2], (MATS,), jnp.float32, math.log(1.0), math.log(4.0))), 1.0, 4.0)
    material_loss = jnp.clip(jax.random.uniform(keys[3], (MATS,), jnp.float32, 0.0, 0.4), 0.0, 0.4)
    source_shift = plant(jax.random.randint(keys[4], (SOURCES, 2), -8, 9), jax.random.fold_in(keys[4], 1), -8, 8).astype(jnp.int32)
    source_mask = plant((jax.random.randint(keys[5], (SOURCES, P_SIZE, Q), 0, 4) < 3).astype(jnp.int32), jax.random.fold_in(keys[5], 1), 0, 1)
    source_weight = jnp.clip(jnp.exp(math.log(4.0) - 2.7725887 * jax.random.uniform(keys[6], (SOURCES,), jnp.float32) ** block_scale(keys[6], (SOURCES,), ((0, 16),), -0.2, 0.2)), 0.25, 4.0)
    return dict(fields=fields, material_map=material_map, material_eps=material_eps, material_loss=material_loss, source_shift=source_shift, source_mask=source_mask, source_weight=source_weight)


COURANT = 0.55
ANGULAR = 0.7
PRECISE = lax.Precision.HIGHEST

def ahead(values, dimension, border):
    remainder = lax.slice_in_dim(values, 1, values.shape[dimension], axis=dimension)
    return jnp.concatenate((remainder, border), dimension)

def behind(values, dimension, border):
    remainder = lax.slice_in_dim(values, 0, values.shape[dimension] - 1, axis=dimension)
    return jnp.concatenate((border, remainder), dimension)

def blank(values, dimension):
    extent = list(values.shape)
    extent[dimension] = 1
    return jnp.zeros(extent, values.dtype)

def magnetic(efield, hfield, borders):

    def change(component, dimension):
        border = borders.get((component, dimension))
        if border is None:
            border = blank(efield[component], dimension)
        return ahead(efield[component], dimension, border) - efield[component]
    new_x = hfield[0] - COURANT * (change(2, 2) - change(1, 0))
    new_y = hfield[1] - COURANT * (change(0, 0) - change(2, 1))
    new_z = hfield[2] - COURANT * (change(1, 1) - change(0, 2))
    return (new_x, new_y, new_z)

def electric(efield, hfield, coef_keep, coef_curl, borders):

    def change(component, dimension):
        border = borders.get((component, dimension))
        if border is None:
            border = blank(hfield[component], dimension)
        return hfield[component] - behind(hfield[component], dimension, border)
    new_x = coef_keep * efield[0] + coef_curl * (change(2, 2) - change(1, 0))
    new_y = coef_keep * efield[1] + coef_curl * (change(0, 0) - change(2, 1))
    new_z = coef_keep * efield[2] + coef_curl * (change(1, 1) - change(0, 2))
    return (new_x, new_y, new_z)

def spectrum(extent, orders, offset, period):
    cell_ids = jnp.arange(extent, dtype=jnp.int32) + offset
    order_ids = jnp.arange(orders, dtype=jnp.int32) - orders // 2
    wrapped = order_ids[:, None] * cell_ids[None, :] % period
    angles = 2.0 * math.pi / period * wrapped.astype(jnp.float32)
    return (jnp.cos(angles), jnp.sin(angles))

def image_tables(pixels, orders_p, orders_q):
    cos_u, sin_u = spectrum(pixels, orders_p, 0, pixels)
    row_table = (jnp.concatenate((cos_u.T, sin_u.T), 1) * (1.0 / math.sqrt(orders_p))).astype(jnp.bfloat16)
    cos_v, sin_v = spectrum(pixels, orders_q, 0, pixels)
    real_v = (cos_v * (1.0 / math.sqrt(orders_q))).astype(jnp.bfloat16)
    imag_v = (sin_v * (1.0 / math.sqrt(orders_q))).astype(jnp.bfloat16)
    g_matrix = jnp.concatenate((jnp.concatenate((real_v, imag_v), 1), jnp.concatenate((-imag_v, real_v), 1)), 0)
    return (row_table, g_matrix)

def source_columns(masked, g_matrix, pixels):
    halves = jnp.concatenate((jnp.concatenate((masked[0, 0], masked[1, 0]), 1), jnp.concatenate((masked[0, 1], masked[1, 1]), 1)), 0)
    spread = jnp.dot(halves, g_matrix, preferred_element_type=jnp.float32).astype(jnp.bfloat16)
    count_p = masked.shape[2]
    real_x = spread[:count_p, :pixels]
    imag_x = spread[:count_p, pixels:]
    real_y = spread[count_p:, :pixels]
    imag_y = spread[count_p:, pixels:]
    upper = jnp.concatenate((real_x, imag_x, real_y, imag_y), 1)
    lower = jnp.concatenate((-imag_x, real_x, -imag_y, real_y), 1)
    return jnp.concatenate((upper, lower), 0)

def reference(fields, material_map, material_eps, material_loss, source_shift, source_mask, source_weight):
    keep_table = (1.0 - material_loss) / (1.0 + material_loss)
    curl_table = COURANT / (material_eps * (1.0 + material_loss))
    coef_keep = keep_table[material_map]
    coef_curl = curl_table[material_map]
    middle = fields.shape[1] // 2
    efield = (fields[0], fields[1], fields[2])
    hfield = (fields[3], fields[4], fields[5])
    zeros_plane = jnp.zeros((2, fields.shape[2], fields.shape[3]), jnp.float32)

    def advance(turn_index, state_now):
        efield, hfield, phase_re, phase_im = state_now
        hfield = magnetic(efield, hfield, {})
        efield = electric(efield, hfield, coef_keep, coef_curl, {})
        moment = jnp.float32(ANGULAR) * (turn_index + 1).astype(jnp.float32)
        monitor = jnp.stack((efield[0][middle], efield[1][middle]))
        phase_re = phase_re + monitor * jnp.cos(moment)
        phase_im = phase_im - monitor * jnp.sin(moment)
        return (efield, hfield, phase_re, phase_im)
    efield, hfield, phase_re, phase_im = lax.fori_loop(0, STEPS, advance, (efield, hfield, zeros_plane, zeros_plane))
    final_fields = jnp.stack(efield + hfield)
    cos_x, sin_x = spectrum(NX, P_SIZE, 0, NX)
    cos_y, sin_y = spectrum(NY, Q, 0, NY)
    part_re = jnp.einsum('cxy,qy->cxq', phase_re, cos_y, precision=PRECISE) + jnp.einsum('cxy,qy->cxq', phase_im, sin_y, precision=PRECISE)
    part_im = jnp.einsum('cxy,qy->cxq', phase_im, cos_y, precision=PRECISE) - jnp.einsum('cxy,qy->cxq', phase_re, sin_y, precision=PRECISE)
    order_re = jnp.einsum('px,cxq->cpq', cos_x, part_re, precision=PRECISE) + jnp.einsum('px,cxq->cpq', sin_x, part_im, precision=PRECISE)
    order_im = jnp.einsum('px,cxq->cpq', cos_x, part_im, precision=PRECISE) - jnp.einsum('px,cxq->cpq', sin_x, part_re, precision=PRECISE)
    scaling = 1.0 / math.sqrt(NX * NY * STEPS)
    orders_b = (jnp.stack((order_re, order_im)) * scaling).astype(jnp.bfloat16)
    row_table, g_matrix = image_tables(M, P_SIZE, Q)

    def add_source(running, inputs):
        offsets, passed, weight = inputs
        rolled = jnp.roll(orders_b, (-offsets[0], -offsets[1]), axis=(2, 3))
        masked = rolled * passed.astype(jnp.bfloat16)
        columns = source_columns(masked, g_matrix, M)
        fields_img = jnp.dot(row_table, columns, preferred_element_type=jnp.float32)
        squared = fields_img * fields_img
        bright = squared.reshape(M, 4, M).sum(axis=1)
        return (running + weight / SOURCES * bright, None)
    image, unused = lax.scan(add_source, jnp.zeros((M, M), jnp.float32), (source_shift, source_mask, source_weight))
    return (final_fields, image)
```

```python
import functools
import math

import jax
import jax.numpy as jnp
import numpy as np
from jax import lax
from jax.experimental import pallas as pl
from jax.experimental.pallas import tpu as pltpu
from jax.sharding import PartitionSpec as P

STEPS = 12
M = 512
COURANT = 0.55
ANGULAR = 0.7
PRECISE = lax.Precision.HIGHEST
MESH = pl.DeviceIdType.MESH


def peer_at(index, tiles_y):
    return {"gx": index // tiles_y, "gy": lax.rem(index, tiles_y)}


def greet(me, count, tiles_y):
    barrier = pltpu.get_barrier_semaphore()

    def signal(k, unused):
        pl.semaphore_signal(
            barrier,
            inc=1,
            device_id=peer_at(lax.rem(me + k, count), tiles_y),
            device_id_type=MESH,
        )
        return unused

    lax.fori_loop(1, count, signal, 0)
    pl.semaphore_wait(barrier, count - 1)


def march(
    tiles_x,
    tiles_y,
    fields_ref,
    material_ref,
    eps_ref,
    loss_ref,
    wave_ref,
    final_ref,
    phasor_ref,
    e_ref,
    h_ref,
    keep_ref,
    curl_ref,
    row_out,
    row_e,
    row_h,
    col_out,
    col_e,
    col_h,
    phase,
    gathered,
    send_sem,
    recv_sem,
    gather_send,
    gather_recv,
):
    count = tiles_x * tiles_y
    depth, cells_x, cells_y = fields_ref.shape[1:]
    middle = depth // 2
    at_x = lax.axis_index("gx")
    at_y = lax.axis_index("gy")
    me = at_x * tiles_y + at_y
    tile = (cells_x, cells_y)
    row_id = lax.broadcasted_iota(jnp.int32, tile, 0)
    col_id = lax.broadcasted_iota(jnp.int32, tile, 1)
    last_row = row_id == cells_x - 1
    first_row = row_id == 0
    last_col = col_id == cells_y - 1
    first_col = col_id == 0
    blank = jnp.zeros(tile, jnp.float32)

    has_right_x = at_x < tiles_x - 1
    has_left_x = at_x > 0
    has_right_y = at_y < tiles_y - 1
    has_left_y = at_y > 0
    routes = (
        (row_out.at[0], row_e, {"gx": at_x - 1}, has_left_x, has_right_x),
        (col_out.at[0], col_e, {"gy": at_y - 1}, has_left_y, has_right_y),
        (row_out.at[1], row_h, {"gx": at_x + 1}, has_right_x, has_left_x),
        (col_out.at[1], col_h, {"gy": at_y + 1}, has_right_y, has_left_y),
    )

    def copy_of(slot):
        source, target, device, _, _ = routes[slot]
        return pltpu.make_async_remote_copy(
            src_ref=source,
            dst_ref=target,
            send_sem=send_sem.at[slot],
            recv_sem=recv_sem.at[slot],
            device_id=device,
            device_id_type=MESH,
        )

    def send(slot):
        @pl.when(routes[slot][3])
        def _():
            copy_of(slot).start()

    def sent(slot):
        @pl.when(routes[slot][3])
        def _():
            copy_of(slot).wait_send()

    def arrived(slot):
        @pl.when(routes[slot][4])
        def _():
            copy_of(slot).wait_recv()

    for halo in (row_e, row_h, col_e, col_h):
        halo[...] = jnp.zeros(halo.shape, jnp.float32)
    greet(me, count, tiles_y)

    keep_values = []
    curl_values = []
    for material in range(eps_ref.shape[0]):
        loss = jnp.full(tile, loss_ref[material], jnp.float32)
        eps = jnp.full(tile, eps_ref[material], jnp.float32)
        keep_values.append((1.0 - loss) / (1.0 + loss))
        curl_values.append(COURANT / (eps * (1.0 + loss)))
    for component in range(3):
        e_ref[component, depth] = blank
        h_ref[component, 0] = blank
    phase[...] = jnp.zeros(phase.shape, jnp.float32)

    def pack_columns(packed, z, first, second, column):
        packed = jnp.where(
            col_id == z, jnp.broadcast_to(first[:, column : column + 1], tile), packed
        )
        return jnp.where(
            col_id == depth + z,
            jnp.broadcast_to(second[:, column : column + 1], tile),
            packed,
        )

    def load(z, packed):
        materials = material_ref[z]
        keep = keep_values[0]
        curl = curl_values[0]
        for material in range(1, len(keep_values)):
            keep = jnp.where(materials == material, keep_values[material], keep)
            curl = jnp.where(materials == material, curl_values[material], curl)
        keep_ref[z] = keep
        curl_ref[z] = curl
        for component in range(3):
            e_ref[component, z] = fields_ref[component, z]
            h_ref[component, z + 1] = fields_ref[3 + component, z]
        row_out[0, 0, pl.ds(z, 1), :] = fields_ref[2, z][0:1]
        row_out[0, 1, pl.ds(z, 1), :] = fields_ref[1, z][0:1]
        return pack_columns(packed, z, fields_ref[2, z], fields_ref[0, z], 0)

    col_out[0] = lax.fori_loop(0, depth, load, blank, unroll=True)
    send(0)
    send(1)

    def step(turn, unused):
        arrived(0)
        arrived(1)
        edge = col_e[...]

        @pl.when(turn > 0)
        def _():
            sent(2)
            sent(3)

        def magnetic(z, packed):
            ex, ey, ez = e_ref[0, z], e_ref[1, z], e_ref[2, z]
            ex_up, ey_up = e_ref[0, z + 1], e_ref[1, z + 1]
            row_z = jnp.broadcast_to(row_e[0, pl.ds(z, 1), :], tile)
            row_y = jnp.broadcast_to(row_e[1, pl.ds(z, 1), :], tile)
            col_z = pltpu.roll(edge, cells_y - 1 - z, 1)
            col_x = pltpu.roll(edge, cells_y - 1 - depth - z, 1)
            dx_ez = jnp.where(last_row, row_z, pltpu.roll(ez, cells_x - 1, 0)) - ez
            dx_ey = jnp.where(last_row, row_y, pltpu.roll(ey, cells_x - 1, 0)) - ey
            dy_ez = jnp.where(last_col, col_z, pltpu.roll(ez, cells_y - 1, 1)) - ez
            dy_ex = jnp.where(last_col, col_x, pltpu.roll(ex, cells_y - 1, 1)) - ex
            hx = h_ref[0, z + 1] - COURANT * (dy_ez - (ey_up - ey))
            hy = h_ref[1, z + 1] - COURANT * ((ex_up - ex) - dx_ez)
            hz = h_ref[2, z + 1] - COURANT * (dx_ey - dy_ex)
            h_ref[0, z + 1] = hx
            h_ref[1, z + 1] = hy
            h_ref[2, z + 1] = hz
            row_out[1, 0, pl.ds(z, 1), :] = hz[cells_x - 1 : cells_x]
            row_out[1, 1, pl.ds(z, 1), :] = hy[cells_x - 1 : cells_x]
            return pack_columns(packed, z, hz, hx, cells_y - 1)

        col_out[1] = lax.fori_loop(0, depth, magnetic, blank, unroll=True)
        send(2)
        send(3)
        sent(0)
        sent(1)
        arrived(2)
        arrived(3)
        edge = col_h[...]

        def electric(z, packed):
            hx, hy, hz = h_ref[0, z + 1], h_ref[1, z + 1], h_ref[2, z + 1]
            hx_down, hy_down = h_ref[0, z], h_ref[1, z]
            row_z = jnp.broadcast_to(row_h[0, pl.ds(z, 1), :], tile)
            row_y = jnp.broadcast_to(row_h[1, pl.ds(z, 1), :], tile)
            col_z = pltpu.roll(edge, lax.rem(cells_y - z, cells_y), 1)
            col_x = pltpu.roll(edge, cells_y - depth - z, 1)
            dx_hz = hz - jnp.where(first_row, row_z, pltpu.roll(hz, 1, 0))
            dx_hy = hy - jnp.where(first_row, row_y, pltpu.roll(hy, 1, 0))
            dy_hz = hz - jnp.where(first_col, col_z, pltpu.roll(hz, 1, 1))
            dy_hx = hx - jnp.where(first_col, col_x, pltpu.roll(hx, 1, 1))
            keep, curl = keep_ref[z], curl_ref[z]
            ex = keep * e_ref[0, z] + curl * (dy_hz - (hy - hy_down))
            ey = keep * e_ref[1, z] + curl * ((hx - hx_down) - dx_hz)
            ez = keep * e_ref[2, z] + curl * (dx_hy - dy_hx)
            e_ref[0, z] = ex
            e_ref[1, z] = ey
            e_ref[2, z] = ez
            row_out[0, 0, pl.ds(z, 1), :] = ez[0:1]
            row_out[0, 1, pl.ds(z, 1), :] = ey[0:1]
            return pack_columns(packed, z, ez, ex, 0)

        col_out[0] = lax.fori_loop(0, depth, electric, blank, unroll=True)

        @pl.when(turn < STEPS - 1)
        def _():
            send(0)
            send(1)

        for component in range(2):
            monitor = e_ref[component, middle]
            phase[component] = phase[component] + monitor * wave_ref[0, turn]
            phase[2 + component] = phase[2 + component] - monitor * wave_ref[1, turn]
        return unused

    lax.fori_loop(0, STEPS, step, 0)
    sent(2)
    sent(3)

    def share(k):
        return pltpu.make_async_remote_copy(
            src_ref=phase,
            dst_ref=gathered.at[me],
            send_sem=gather_send.at[k],
            recv_sem=gather_recv.at[k],
            device_id=peer_at(lax.rem(me + k, count), tiles_y),
            device_id_type=MESH,
        )

    def start(k, unused):
        share(k).start()
        return unused

    lax.fori_loop(1, count, start, 0)

    def store(z, unused):
        for component in range(3):
            final_ref[component, z] = e_ref[component, z]
            final_ref[3 + component, z] = h_ref[component, z + 1]
        return unused

    lax.fori_loop(0, depth, store, 0, unroll=True)

    def finish(k, unused):
        share(k).wait_send()
        share(k).wait_recv()
        return unused

    lax.fori_loop(1, count, finish, 0)
    gathered[me] = phase[...]
    for tile_x in range(tiles_x):
        for tile_y in range(tiles_y):
            phasor_ref[
                :,
                tile_x * cells_x : (tile_x + 1) * cells_x,
                tile_y * cells_y : (tile_y + 1) * cells_y,
            ] = gathered[tile_x * tiles_y + tile_y]


def run_march(fields, material_map, material_eps, material_loss, tiles_x, tiles_y):
    depth, cells_x, cells_y = fields.shape[1:]
    count = tiles_x * tiles_y
    moments = np.float32(ANGULAR) * np.arange(1, STEPS + 1, dtype=np.float32)
    wave = jnp.asarray(np.stack((np.cos(moments), np.sin(moments))).astype(np.float32))
    vmem = pl.BlockSpec(memory_space=pltpu.VMEM)
    smem = pl.BlockSpec(memory_space=pltpu.SMEM)
    state = (3, depth + 1, cells_x, cells_y)
    return pl.pallas_call(
        functools.partial(march, tiles_x, tiles_y),
        out_shape=(
            jax.ShapeDtypeStruct(fields.shape, jnp.float32),
            jax.ShapeDtypeStruct((4, cells_x * tiles_x, cells_y * tiles_y), jnp.float32),
        ),
        in_specs=[vmem, vmem, smem, smem, smem],
        out_specs=(vmem, vmem),
        scratch_shapes=[
            pltpu.VMEM(state, jnp.float32),
            pltpu.VMEM(state, jnp.float32),
            pltpu.VMEM((depth, cells_x, cells_y), jnp.float32),
            pltpu.VMEM((depth, cells_x, cells_y), jnp.float32),
            pltpu.VMEM((2, 2, depth, cells_y), jnp.float32),
            pltpu.VMEM((2, depth, cells_y), jnp.float32),
            pltpu.VMEM((2, depth, cells_y), jnp.float32),
            pltpu.VMEM((2, cells_x, cells_y), jnp.float32),
            pltpu.VMEM((cells_x, cells_y), jnp.float32),
            pltpu.VMEM((cells_x, cells_y), jnp.float32),
            pltpu.VMEM((4, cells_x, cells_y), jnp.float32),
            pltpu.VMEM((count, 4, cells_x, cells_y), jnp.float32),
            pltpu.SemaphoreType.DMA((4,)),
            pltpu.SemaphoreType.DMA((4,)),
            pltpu.SemaphoreType.DMA((count,)),
            pltpu.SemaphoreType.DMA((count,)),
        ],
        compiler_params=pltpu.CompilerParams(
            collective_id=0, has_side_effects=True, vmem_limit_bytes=40 * 1024 * 1024
        ),
    )(fields, material_map, material_eps, material_loss, wave)


def picture(
    tiles_x,
    tiles_y,
    orders_ref,
    shift_ref,
    mask_ref,
    weight_ref,
    rows_ref,
    g_ref,
    image_ref,
    columns,
    part,
    landed,
    send_sem,
    recv_sem,
):
    count = tiles_x * tiles_y
    me = lax.axis_index("gx") * tiles_y + lax.axis_index("gy")
    sources = mask_ref.shape[0]
    size_p = mask_ref.shape[1] // 2
    size_q = mask_ref.shape[2] // 2
    pixels = image_ref.shape[1]
    strip = image_ref.shape[0]
    greet(me, count, tiles_y)

    def one_hot(size, offset, flipped):
        to_id = lax.broadcasted_iota(jnp.int32, (2 * size, 2 * size), 1 if flipped else 0)
        from_id = lax.broadcasted_iota(jnp.int32, (2 * size, 2 * size), 0 if flipped else 1)
        to_half = jnp.where(to_id >= size, size, 0)
        moved = to_id - to_half + offset
        moved = jnp.where(moved < 0, moved + size, moved)
        moved = jnp.where(moved >= size, moved - size, moved)
        return jnp.where(from_id == moved + to_half, 1.0, 0.0).astype(jnp.bfloat16)

    def prepare(source, unused):
        pick_p = one_hot(size_p, shift_ref[source, 0], False)
        pick_q = one_hot(size_q, shift_ref[source, 1], True)
        rolled = jnp.dot(pick_p, orders_ref[...], preferred_element_type=jnp.float32)
        rolled = jnp.dot(
            rolled.astype(jnp.bfloat16), pick_q, preferred_element_type=jnp.float32
        )
        masked = (rolled * mask_ref[source].astype(jnp.float32)).astype(jnp.bfloat16)
        spread = jnp.dot(masked, g_ref[...], preferred_element_type=jnp.float32)
        spread = spread.astype(jnp.bfloat16)
        for block in range(2):
            real = spread[block * size_p : (block + 1) * size_p, :pixels]
            imag = spread[block * size_p : (block + 1) * size_p, pixels:]
            at = 2 * block * pixels
            columns[source, :size_p, at : at + pixels] = real
            columns[source, :size_p, at + pixels : at + 2 * pixels] = imag
            columns[source, size_p:, at : at + pixels] = -imag
            columns[source, size_p:, at + pixels : at + 2 * pixels] = real
        return unused

    lax.fori_loop(0, sources, prepare, 0)

    def copy_to(target, k):
        return pltpu.make_async_remote_copy(
            src_ref=part.at[target],
            dst_ref=landed.at[me],
            send_sem=send_sem.at[k],
            recv_sem=recv_sem.at[k],
            device_id=peer_at(target, tiles_y),
            device_id_type=MESH,
        )

    groups = 4 if count % 4 == 0 else 1
    per_group = count // groups
    high = per_group * strip
    scale = 1.0 / (sources * count)

    def one_group(turn, unused):
        group = lax.rem(me // per_group + 1 + turn, groups)
        table = rows_ref[pl.ds(pl.multiple_of(group * high, high), high), :]

        def add_source(source, running):
            bright = None
            for block in range(4):
                values = jnp.dot(
                    table,
                    columns[source, :, block * pixels : (block + 1) * pixels],
                    preferred_element_type=jnp.float32,
                )
                squared = values * values
                bright = squared if bright is None else bright + squared
            return running + (weight_ref[source] * scale) * bright

        total = lax.fori_loop(
            0, sources, add_source, jnp.zeros((high, pixels), jnp.float32)
        )
        for piece in range(per_group):
            part[group * per_group + piece] = total[piece * strip : (piece + 1) * strip]

        def start(piece, unused):
            target = group * per_group + piece

            @pl.when(target != me)
            def _():
                copy_to(target, lax.rem(target - me + count, count)).start()

            return unused

        return lax.fori_loop(0, per_group, start, unused)

    lax.fori_loop(0, groups, one_group, 0)

    def finish(k, unused):
        copy = copy_to(lax.rem(me + k, count), k)
        copy.wait_send()
        copy.wait_recv()
        return unused

    lax.fori_loop(1, count, finish, 0)
    landed[me] = part[me]

    def add(index, running):
        return running + landed[index]

    image_ref[...] = lax.fori_loop(
        0, count, add, jnp.zeros((strip, pixels), jnp.float32)
    )


def run_picture(orders, shift, mask, weight, row_table, g_matrix, tiles_x, tiles_y):
    count = tiles_x * tiles_y
    pixels = row_table.shape[0]
    strip = pixels // count
    vmem = pl.BlockSpec(memory_space=pltpu.VMEM)
    smem = pl.BlockSpec(memory_space=pltpu.SMEM)
    return pl.pallas_call(
        functools.partial(picture, tiles_x, tiles_y),
        out_shape=jax.ShapeDtypeStruct((strip, pixels), jnp.float32),
        in_specs=[vmem, smem, vmem, smem, vmem, vmem],
        out_specs=vmem,
        scratch_shapes=[
            pltpu.VMEM((mask.shape[0], row_table.shape[1], 4 * pixels), jnp.bfloat16),
            pltpu.VMEM((count, strip, pixels), jnp.float32),
            pltpu.VMEM((count, strip, pixels), jnp.float32),
            pltpu.SemaphoreType.DMA((count,)),
            pltpu.SemaphoreType.DMA((count,)),
        ],
        compiler_params=pltpu.CompilerParams(
            collective_id=1, has_side_effects=True, vmem_limit_bytes=48 * 1024 * 1024
        ),
    )(orders, shift, mask, weight, row_table, g_matrix)


def spectrum(extent, orders, period):
    wrapped = ((np.arange(orders) - orders // 2)[:, None] * np.arange(extent)[None, :]) % period
    angles = 2.0 * math.pi / period * wrapped
    return np.cos(angles).astype(np.float32), np.sin(angles).astype(np.float32)


def image_tables(pixels, orders_p, orders_q):
    cos_u, sin_u = spectrum(pixels, orders_p, pixels)
    row_table = np.concatenate((cos_u.T, sin_u.T), 1) * np.float32(1.0 / math.sqrt(orders_p))
    cos_v, sin_v = spectrum(pixels, orders_q, pixels)
    real_v = cos_v * np.float32(1.0 / math.sqrt(orders_q))
    imag_v = sin_v * np.float32(1.0 / math.sqrt(orders_q))
    g_matrix = np.block([[real_v, imag_v], [-imag_v, real_v]])
    return (row_table.astype(jnp.bfloat16), g_matrix.astype(jnp.bfloat16))


def body(
    fields, material_map, material_eps, material_loss, source_shift, source_mask, source_weight
):
    tiles_x = lax.axis_size("gx")
    tiles_y = lax.axis_size("gy")
    orders_p, orders_q = source_mask.shape[1:]
    final_fields, phasor = run_march(
        fields, material_map, material_eps, material_loss, tiles_x, tiles_y
    )
    period_x, period_y = phasor.shape[1:]
    cos_x, sin_x = spectrum(period_x, orders_p, period_x)
    cos_y, sin_y = spectrum(period_y, orders_q, period_y)
    both_y = jnp.asarray(np.concatenate((cos_y, sin_y), 0).T)
    along = jnp.dot(
        phasor.reshape(4 * period_x, period_y), both_y, precision=PRECISE
    ).reshape(2, 2, period_x, 2 * orders_q)
    part_re = along[0, :, :, :orders_q] + along[1, :, :, orders_q:]
    part_im = along[1, :, :, :orders_q] - along[0, :, :, orders_q:]
    both_x = jnp.asarray(np.concatenate((cos_x, sin_x), 1))
    stacked = jnp.concatenate(
        (
            jnp.concatenate((part_re, part_im), 2),
            jnp.concatenate((part_im, -part_re), 2),
        ),
        1,
    )
    orders = jnp.einsum("px,cxq->cpq", both_x, stacked, precision=PRECISE)
    scaling = 1.0 / math.sqrt(period_x * period_y * STEPS)
    orders_b = (orders * scaling).astype(jnp.bfloat16).reshape(2 * orders_p, 2 * orders_q)
    row_table, g_matrix = image_tables(M, orders_p, orders_q)
    mask = jnp.tile(source_mask.astype(jnp.bfloat16), (1, 2, 2))
    image = run_picture(
        orders_b,
        source_shift,
        mask,
        source_weight,
        jnp.asarray(row_table),
        jnp.asarray(g_matrix),
        tiles_x,
        tiles_y,
    )
    return (final_fields, image)


def solution(mesh):
    placed = (
        P("clips", None, "gx", "gy"),
        P("clips", "gx", "gy"),
        P(),
        P(),
        P(("gx", "gy"), None),
        P(("gx", "gy"), None, None),
        P(("gx", "gy")),
    )
    return jax.shard_map(
        body,
        mesh=mesh,
        in_specs=placed,
        out_specs=(P("clips", None, "gx", "gy"), P(("gx", "gy"), "clips")),
        check_vma=False,
    )
```

```python
import functools
import math

import jax
import jax.numpy as jnp
import numpy as np
from jax import lax
from jax.experimental import pallas as pl
from jax.experimental.pallas import tpu as pltpu
from jax.sharding import PartitionSpec as P

STEPS = 12
M = 512
COURANT = 0.55
ANGULAR = 0.7
PRECISE = lax.Precision.HIGHEST
MESH = pl.DeviceIdType.MESH
GROUP = 8


def peer_at(index, tiles_y):
    return {"gx": index // tiles_y, "gy": lax.rem(index, tiles_y)}


def greet(me, count, tiles_y):
    barrier = pltpu.get_barrier_semaphore()

    def signal(k, unused):
        pl.semaphore_signal(
            barrier,
            inc=1,
            device_id=peer_at(lax.rem(me + k, count), tiles_y),
            device_id_type=MESH,
        )
        return unused

    lax.fori_loop(1, count, signal, 0)
    pl.semaphore_wait(barrier, count - 1)


def march(
    tiles_x,
    tiles_y,
    fields_ref,
    material_ref,
    eps_ref,
    loss_ref,
    wave_ref,
    final_ref,
    phasor_ref,
    e_ref,
    h_ref,
    keep_ref,
    curl_ref,
    row_out,
    row_e,
    row_h,
    col_out,
    col_e,
    col_h,
    phase,
    gathered,
    send_sem,
    recv_sem,
    gather_send,
    gather_recv,
):
    count = tiles_x * tiles_y
    depth, cells_x, cells_y = fields_ref.shape[1:]
    middle = depth // 2
    at_x = lax.axis_index("gx")
    at_y = lax.axis_index("gy")
    me = at_x * tiles_y + at_y
    tile = (cells_x, cells_y)
    row_id = lax.broadcasted_iota(jnp.int32, tile, 0)
    col_id = lax.broadcasted_iota(jnp.int32, tile, 1)
    last_row = row_id == cells_x - 1
    first_row = row_id == 0
    last_col = col_id == cells_y - 1
    first_col = col_id == 0
    blank = jnp.zeros(tile, jnp.float32)

    has_right_x = at_x < tiles_x - 1
    has_left_x = at_x > 0
    has_right_y = at_y < tiles_y - 1
    has_left_y = at_y > 0
    routes = (
        (row_out.at[0], row_e, {"gx": at_x - 1}, has_left_x, has_right_x),
        (col_out.at[0], col_e, {"gy": at_y - 1}, has_left_y, has_right_y),
        (row_out.at[1], row_h, {"gx": at_x + 1}, has_right_x, has_left_x),
        (col_out.at[1], col_h, {"gy": at_y + 1}, has_right_y, has_left_y),
    )

    def copy_of(slot):
        source, target, device, _, _ = routes[slot]
        return pltpu.make_async_remote_copy(
            src_ref=source,
            dst_ref=target,
            send_sem=send_sem.at[slot],
            recv_sem=recv_sem.at[slot],
            device_id=device,
            device_id_type=MESH,
        )

    def send(slot):
        @pl.when(routes[slot][3])
        def _():
            copy_of(slot).start()

    def sent(slot):
        @pl.when(routes[slot][3])
        def _():
            copy_of(slot).wait_send()

    def arrived(slot):
        @pl.when(routes[slot][4])
        def _():
            copy_of(slot).wait_recv()

    for halo in (row_e, row_h, col_e, col_h):
        halo[...] = jnp.zeros(halo.shape, jnp.float32)
    greet(me, count, tiles_y)

    keep_values = []
    curl_values = []
    for material in range(eps_ref.shape[0]):
        loss = jnp.full(tile, loss_ref[material], jnp.float32)
        eps = jnp.full(tile, eps_ref[material], jnp.float32)
        keep_values.append((1.0 - loss) / (1.0 + loss))
        curl_values.append(COURANT / (eps * (1.0 + loss)))
    for component in range(3):
        e_ref[component, depth] = blank
        h_ref[component, 0] = blank
    phase[...] = jnp.zeros(phase.shape, jnp.float32)

    def pack_columns(packed, z, first, second, column):
        packed = jnp.where(
            col_id == z, jnp.broadcast_to(first[:, column : column + 1], tile), packed
        )
        return jnp.where(
            col_id == depth + z,
            jnp.broadcast_to(second[:, column : column + 1], tile),
            packed,
        )

    def load(z, packed):
        materials = material_ref[z]
        keep = keep_values[0]
        curl = curl_values[0]
        for material in range(1, len(keep_values)):
            keep = jnp.where(materials == material, keep_values[material], keep)
            curl = jnp.where(materials == material, curl_values[material], curl)
        keep_ref[z] = keep
        curl_ref[z] = curl
        for component in range(3):
            e_ref[component, z] = fields_ref[component, z]
            h_ref[component, z + 1] = fields_ref[3 + component, z]
        row_out[0, 0, pl.ds(z, 1), :] = fields_ref[2, z][0:1]
        row_out[0, 1, pl.ds(z, 1), :] = fields_ref[1, z][0:1]
        return pack_columns(packed, z, fields_ref[2, z], fields_ref[0, z], 0)

    col_out[0] = lax.fori_loop(0, depth, load, blank, unroll=True)
    send(0)
    send(1)

    def step(turn, unused):
        arrived(0)
        arrived(1)
        edge = col_e[...]

        @pl.when(turn > 0)
        def _():
            sent(2)
            sent(3)

        def magnetic(block, packed):
            base = block * GROUP
            ex = [e_ref[0, base + j] for j in range(GROUP + 1)]
            ey = [e_ref[1, base + j] for j in range(GROUP + 1)]
            ez = [e_ref[2, base + j] for j in range(GROUP)]
            new = []
            for j in range(GROUP):
                z = base + j
                row_z = jnp.broadcast_to(row_e[0, pl.ds(z, 1), :], tile)
                row_y = jnp.broadcast_to(row_e[1, pl.ds(z, 1), :], tile)
                col_z = pltpu.roll(edge, cells_y - 1 - z, 1)
                col_x = pltpu.roll(edge, cells_y - 1 - depth - z, 1)
                dx_ez = jnp.where(last_row, row_z, pltpu.roll(ez[j], cells_x - 1, 0)) - ez[j]
                dx_ey = jnp.where(last_row, row_y, pltpu.roll(ey[j], cells_x - 1, 0)) - ey[j]
                dy_ez = jnp.where(last_col, col_z, pltpu.roll(ez[j], cells_y - 1, 1)) - ez[j]
                dy_ex = jnp.where(last_col, col_x, pltpu.roll(ex[j], cells_y - 1, 1)) - ex[j]
                hx = h_ref[0, z + 1] - COURANT * (dy_ez - (ey[j + 1] - ey[j]))
                hy = h_ref[1, z + 1] - COURANT * ((ex[j + 1] - ex[j]) - dx_ez)
                hz = h_ref[2, z + 1] - COURANT * (dx_ey - dy_ex)
                new.append((hx, hy, hz))
            for j in range(GROUP):
                z = base + j
                hx, hy, hz = new[j]
                h_ref[0, z + 1] = hx
                h_ref[1, z + 1] = hy
                h_ref[2, z + 1] = hz
                row_out[1, 0, pl.ds(z, 1), :] = hz[cells_x - 1 : cells_x]
                row_out[1, 1, pl.ds(z, 1), :] = hy[cells_x - 1 : cells_x]
                packed = pack_columns(packed, z, hz, hx, cells_y - 1)
            return packed

        col_out[1] = lax.fori_loop(0, depth // GROUP, magnetic, blank, unroll=True)
        send(2)
        send(3)
        sent(0)
        sent(1)
        arrived(2)
        arrived(3)
        edge = col_h[...]

        def electric(block, packed):
            base = block * GROUP
            hx = [h_ref[0, base + j] for j in range(GROUP + 1)]
            hy = [h_ref[1, base + j] for j in range(GROUP + 1)]
            hz = [None] + [h_ref[2, base + j + 1] for j in range(GROUP)]
            new = []
            for j in range(1, GROUP + 1):
                z = base + j - 1
                row_z = jnp.broadcast_to(row_h[0, pl.ds(z, 1), :], tile)
                row_y = jnp.broadcast_to(row_h[1, pl.ds(z, 1), :], tile)
                col_z = pltpu.roll(edge, lax.rem(cells_y - z, cells_y), 1)
                col_x = pltpu.roll(edge, cells_y - depth - z, 1)
                dx_hz = hz[j] - jnp.where(first_row, row_z, pltpu.roll(hz[j], 1, 0))
                dx_hy = hy[j] - jnp.where(first_row, row_y, pltpu.roll(hy[j], 1, 0))
                dy_hz = hz[j] - jnp.where(first_col, col_z, pltpu.roll(hz[j], 1, 1))
                dy_hx = hx[j] - jnp.where(first_col, col_x, pltpu.roll(hx[j], 1, 1))
                keep, curl = keep_ref[z], curl_ref[z]
                ex = keep * e_ref[0, z] + curl * (dy_hz - (hy[j] - hy[j - 1]))
                ey = keep * e_ref[1, z] + curl * ((hx[j] - hx[j - 1]) - dx_hz)
                ez = keep * e_ref[2, z] + curl * (dx_hy - dy_hx)
                new.append((ex, ey, ez))
            for j in range(GROUP):
                z = base + j
                ex, ey, ez = new[j]
                e_ref[0, z] = ex
                e_ref[1, z] = ey
                e_ref[2, z] = ez
                row_out[0, 0, pl.ds(z, 1), :] = ez[0:1]
                row_out[0, 1, pl.ds(z, 1), :] = ey[0:1]
                packed = pack_columns(packed, z, ez, ex, 0)
            return packed

        col_out[0] = lax.fori_loop(0, depth // GROUP, electric, blank, unroll=True)

        @pl.when(turn < STEPS - 1)
        def _():
            send(0)
            send(1)

        for component in range(2):
            monitor = e_ref[component, middle]
            phase[component] = phase[component] + monitor * wave_ref[0, turn]
            phase[2 + component] = phase[2 + component] - monitor * wave_ref[1, turn]
        return unused

    lax.fori_loop(0, STEPS, step, 0)
    sent(2)
    sent(3)

    def share(k):
        return pltpu.make_async_remote_copy(
            src_ref=phase,
            dst_ref=gathered.at[me],
            send_sem=gather_send.at[k],
            recv_sem=gather_recv.at[k],
            device_id=peer_at(lax.rem(me + k, count), tiles_y),
            device_id_type=MESH,
        )

    def start(k, unused):
        share(k).start()
        return unused

    lax.fori_loop(1, count, start, 0)

    def store(z, unused):
        for component in range(3):
            final_ref[component, z] = e_ref[component, z]
            final_ref[3 + component, z] = h_ref[component, z + 1]
        return unused

    lax.fori_loop(0, depth, store, 0, unroll=True)

    def finish(k, unused):
        share(k).wait_send()
        share(k).wait_recv()
        return unused

    lax.fori_loop(1, count, finish, 0)
    gathered[me] = phase[...]
    for tile_x in range(tiles_x):
        for tile_y in range(tiles_y):
            phasor_ref[
                :,
                tile_x * cells_x : (tile_x + 1) * cells_x,
                tile_y * cells_y : (tile_y + 1) * cells_y,
            ] = gathered[tile_x * tiles_y + tile_y]


def run_march(fields, material_map, material_eps, material_loss, tiles_x, tiles_y):
    depth, cells_x, cells_y = fields.shape[1:]
    count = tiles_x * tiles_y
    moments = np.float32(ANGULAR) * np.arange(1, STEPS + 1, dtype=np.float32)
    wave = jnp.asarray(np.stack((np.cos(moments), np.sin(moments))).astype(np.float32))
    vmem = pl.BlockSpec(memory_space=pltpu.VMEM)
    smem = pl.BlockSpec(memory_space=pltpu.SMEM)
    state = (3, depth + 1, cells_x, cells_y)
    return pl.pallas_call(
        functools.partial(march, tiles_x, tiles_y),
        out_shape=(
            jax.ShapeDtypeStruct(fields.shape, jnp.float32),
            jax.ShapeDtypeStruct((4, cells_x * tiles_x, cells_y * tiles_y), jnp.float32),
        ),
        in_specs=[vmem, vmem, smem, smem, smem],
        out_specs=(vmem, vmem),
        scratch_shapes=[
            pltpu.VMEM(state, jnp.float32),
            pltpu.VMEM(state, jnp.float32),
            pltpu.VMEM((depth, cells_x, cells_y), jnp.float32),
            pltpu.VMEM((depth, cells_x, cells_y), jnp.float32),
            pltpu.VMEM((2, 2, depth, cells_y), jnp.float32),
            pltpu.VMEM((2, depth, cells_y), jnp.float32),
            pltpu.VMEM((2, depth, cells_y), jnp.float32),
            pltpu.VMEM((2, cells_x, cells_y), jnp.float32),
            pltpu.VMEM((cells_x, cells_y), jnp.float32),
            pltpu.VMEM((cells_x, cells_y), jnp.float32),
            pltpu.VMEM((4, cells_x, cells_y), jnp.float32),
            pltpu.VMEM((count, 4, cells_x, cells_y), jnp.float32),
            pltpu.SemaphoreType.DMA((4,)),
            pltpu.SemaphoreType.DMA((4,)),
            pltpu.SemaphoreType.DMA((count,)),
            pltpu.SemaphoreType.DMA((count,)),
        ],
        compiler_params=pltpu.CompilerParams(
            collective_id=0, has_side_effects=True, vmem_limit_bytes=40 * 1024 * 1024
        ),
    )(fields, material_map, material_eps, material_loss, wave)


def picture(
    tiles_x,
    tiles_y,
    orders_ref,
    shift_ref,
    mask_ref,
    weight_ref,
    rows_ref,
    g_ref,
    image_ref,
    columns,
    part,
    swapped,
    crossed,
    strips,
    landed,
    swap_send,
    swap_recv,
    cross_send,
    cross_recv,
    hand_send,
    hand_recv,
):
    count = tiles_x * tiles_y
    me = lax.axis_index("gx") * tiles_y + lax.axis_index("gy")
    sources = mask_ref.shape[0]
    size_p = mask_ref.shape[1] // 2
    size_q = mask_ref.shape[2] // 2
    pixels = image_ref.shape[1]
    strip = image_ref.shape[0]
    greet(me, count, tiles_y)

    def one_hot(size, offset, flipped):
        to_id = lax.broadcasted_iota(jnp.int32, (2 * size, 2 * size), 1 if flipped else 0)
        from_id = lax.broadcasted_iota(jnp.int32, (2 * size, 2 * size), 0 if flipped else 1)
        to_half = jnp.where(to_id >= size, size, 0)
        moved = to_id - to_half + offset
        moved = jnp.where(moved < 0, moved + size, moved)
        moved = jnp.where(moved >= size, moved - size, moved)
        return jnp.where(from_id == moved + to_half, 1.0, 0.0).astype(jnp.bfloat16)

    def prepare(source, unused):
        pick_p = one_hot(size_p, shift_ref[source, 0], False)
        pick_q = one_hot(size_q, shift_ref[source, 1], True)
        rolled = jnp.dot(pick_p, orders_ref[...], preferred_element_type=jnp.float32)
        rolled = jnp.dot(
            rolled.astype(jnp.bfloat16), pick_q, preferred_element_type=jnp.float32
        )
        masked = (rolled * mask_ref[source].astype(jnp.float32)).astype(jnp.bfloat16)
        spread = jnp.dot(masked, g_ref[...], preferred_element_type=jnp.float32)
        spread = spread.astype(jnp.bfloat16)
        for block in range(2):
            real = spread[block * size_p : (block + 1) * size_p, :pixels]
            imag = spread[block * size_p : (block + 1) * size_p, pixels:]
            at = 2 * block * pixels
            columns[source, :size_p, at : at + pixels] = real
            columns[source, :size_p, at + pixels : at + 2 * pixels] = imag
            columns[source, size_p:, at : at + pixels] = -imag
            columns[source, size_p:, at + pixels : at + 2 * pixels] = real
        return unused

    lax.fori_loop(0, sources, prepare, 0)

    pairs = tiles_x // 2
    at_x = lax.axis_index("gx")
    at_y = lax.axis_index("gy")
    core = lax.rem(at_x, 2)
    at_pair = at_x // 2
    scale = 1.0 / (sources * count)
    high = tiles_y * strip

    def render(pair, half):
        table = rows_ref[
            pl.ds(pl.multiple_of((2 * pair + half) * high, high), high), :
        ]
        total = jnp.zeros((high, pixels), jnp.float32)
        for source in range(sources):
            bright = None
            for block in range(4):
                values = jnp.dot(
                    table,
                    columns[source, :, block * pixels : (block + 1) * pixels],
                    preferred_element_type=jnp.float32,
                )
                squared = values * values
                bright = squared if bright is None else bright + squared
            total = total + (weight_ref[source] * scale) * bright
        part[pair, half] = total

    def swap(pair):
        return pltpu.make_async_remote_copy(
            src_ref=part.at[pair, 1 - core],
            dst_ref=swapped.at[pair],
            send_sem=swap_send.at[pair],
            recv_sem=swap_recv.at[pair],
            device_id={"gx": at_x + 1 - 2 * core},
            device_id_type=MESH,
        )

    def cross(k):
        pair = lax.rem(at_pair + k, pairs)
        return pltpu.make_async_remote_copy(
            src_ref=part.at[pair, core],
            dst_ref=crossed.at[k],
            send_sem=cross_send.at[k],
            recv_sem=cross_recv.at[k],
            device_id={"gx": 2 * pair + core},
            device_id_type=MESH,
        )

    def away(k):
        return lax.rem(at_pair + k, pairs)

    def first(turn, unused):
        pair = away(turn + 1)
        render(pair, 1 - core)
        swap(pair).start()
        render(pair, core)
        return unused

    lax.fori_loop(0, pairs, first, 0)

    def second(turn, unused):
        pair = away(turn + 1)
        swap(pair).wait_recv()
        part[pair, core] = part[pair, core] + swapped[pair]

        @pl.when(turn < pairs - 1)
        def _():
            cross(turn + 1).start()

        return unused

    lax.fori_loop(0, pairs, second, 0)

    def gather_pairs(k, running):
        cross(k).wait_recv()
        return running + crossed[k]

    mine = lax.fori_loop(1, pairs, gather_pairs, part[at_pair, core])
    for owner in range(tiles_y):
        strips[owner] = mine[owner * strip : (owner + 1) * strip]

    def hand(k):
        owner = lax.rem(at_y + k, tiles_y)
        return pltpu.make_async_remote_copy(
            src_ref=strips.at[owner],
            dst_ref=landed.at[k],
            send_sem=hand_send.at[k],
            recv_sem=hand_recv.at[k],
            device_id={"gy": owner},
            device_id_type=MESH,
        )

    for k in range(1, tiles_y):
        hand(k).start()
    total = strips[at_y]
    for k in range(1, tiles_y):
        hand(k).wait_recv()
        total = total + landed[k]
    image_ref[...] = total
    for k in range(1, tiles_y):
        hand(k).wait_send()

    def finish(pair, unused):
        swap(pair).wait_send()

        @pl.when(pair > 0)
        def _():
            cross(pair).wait_send()

        return unused

    lax.fori_loop(0, pairs, finish, 0)


def run_picture(orders, shift, mask, weight, row_table, g_matrix, tiles_x, tiles_y):
    count = tiles_x * tiles_y
    pixels = row_table.shape[0]
    strip = pixels // count
    pairs = tiles_x // 2
    vmem = pl.BlockSpec(memory_space=pltpu.VMEM)
    smem = pl.BlockSpec(memory_space=pltpu.SMEM)
    return pl.pallas_call(
        functools.partial(picture, tiles_x, tiles_y),
        out_shape=jax.ShapeDtypeStruct((strip, pixels), jnp.float32),
        in_specs=[vmem, smem, vmem, smem, vmem, vmem],
        out_specs=vmem,
        scratch_shapes=[
            pltpu.VMEM((mask.shape[0], row_table.shape[1], 4 * pixels), jnp.bfloat16),
            pltpu.VMEM((pairs, 2, tiles_y * strip, pixels), jnp.float32),
            pltpu.VMEM((pairs, tiles_y * strip, pixels), jnp.float32),
            pltpu.VMEM((pairs, tiles_y * strip, pixels), jnp.float32),
            pltpu.VMEM((tiles_y, strip, pixels), jnp.float32),
            pltpu.VMEM((tiles_y, strip, pixels), jnp.float32),
        ]
        + [pltpu.SemaphoreType.DMA((pairs,))] * 4
        + [pltpu.SemaphoreType.DMA((tiles_y,))] * 2,
        compiler_params=pltpu.CompilerParams(
            collective_id=1, has_side_effects=True, vmem_limit_bytes=48 * 1024 * 1024
        ),
    )(orders, shift, mask, weight, row_table, g_matrix)


def spectrum(extent, orders, period):
    wrapped = ((np.arange(orders) - orders // 2)[:, None] * np.arange(extent)[None, :]) % period
    angles = 2.0 * math.pi / period * wrapped
    return np.cos(angles).astype(np.float32), np.sin(angles).astype(np.float32)


def image_tables(pixels, orders_p, orders_q):
    cos_u, sin_u = spectrum(pixels, orders_p, pixels)
    row_table = np.concatenate((cos_u.T, sin_u.T), 1) * np.float32(1.0 / math.sqrt(orders_p))
    cos_v, sin_v = spectrum(pixels, orders_q, pixels)
    real_v = cos_v * np.float32(1.0 / math.sqrt(orders_q))
    imag_v = sin_v * np.float32(1.0 / math.sqrt(orders_q))
    g_matrix = np.block([[real_v, imag_v], [-imag_v, real_v]])
    return (row_table.astype(jnp.bfloat16), g_matrix.astype(jnp.bfloat16))


def body(
    fields, material_map, material_eps, material_loss, source_shift, source_mask, source_weight
):
    tiles_x = lax.axis_size("gx")
    tiles_y = lax.axis_size("gy")
    orders_p, orders_q = source_mask.shape[1:]
    final_fields, phasor = run_march(
        fields, material_map, material_eps, material_loss, tiles_x, tiles_y
    )
    period_x, period_y = phasor.shape[1:]
    cos_x, sin_x = spectrum(period_x, orders_p, period_x)
    cos_y, sin_y = spectrum(period_y, orders_q, period_y)
    both_y = jnp.asarray(np.concatenate((cos_y, sin_y), 0).T)
    along = jnp.dot(
        phasor.reshape(4 * period_x, period_y), both_y, precision=PRECISE
    ).reshape(2, 2, period_x, 2 * orders_q)
    part_re = along[0, :, :, :orders_q] + along[1, :, :, orders_q:]
    part_im = along[1, :, :, :orders_q] - along[0, :, :, orders_q:]
    both_x = jnp.asarray(np.concatenate((cos_x, sin_x), 1))
    stacked = jnp.concatenate(
        (
            jnp.concatenate((part_re, part_im), 2),
            jnp.concatenate((part_im, -part_re), 2),
        ),
        1,
    )
    orders = jnp.einsum("px,cxq->cpq", both_x, stacked, precision=PRECISE)
    scaling = 1.0 / math.sqrt(period_x * period_y * STEPS)
    orders_b = (orders * scaling).astype(jnp.bfloat16).reshape(2 * orders_p, 2 * orders_q)
    row_table, g_matrix = image_tables(M, orders_p, orders_q)
    mask = jnp.tile(source_mask.astype(jnp.bfloat16), (1, 2, 2))
    image = run_picture(
        orders_b,
        source_shift,
        mask,
        source_weight,
        jnp.asarray(row_table),
        jnp.asarray(g_matrix),
        tiles_x,
        tiles_y,
    )
    return (final_fields, image)


def solution(mesh):
    placed = (
        P("clips", None, "gx", "gy"),
        P("clips", "gx", "gy"),
        P(),
        P(),
        P(("gx", "gy"), None),
        P(("gx", "gy"), None, None),
        P(("gx", "gy")),
    )
    return jax.shard_map(
        body,
        mesh=mesh,
        in_specs=placed,
        out_specs=(P("clips", None, "gx", "gy"), P(("gx", "gy"), "clips")),
        check_vma=False,
    )
```

```python
import functools
import math

import jax
import jax.numpy as jnp
import numpy as np
from jax import lax
from jax.experimental import pallas as pl
from jax.experimental.pallas import tpu as pltpu
from jax.sharding import PartitionSpec as P

STEPS = 12
M = 512
COURANT = 0.55
ANGULAR = 0.7
PRECISE = lax.Precision.HIGHEST
MESH = pl.DeviceIdType.MESH
GROUP = 8


def peer_at(index, tiles_y):
    return {"gx": index // tiles_y, "gy": lax.rem(index, tiles_y)}


def greet(me, count, tiles_y):
    barrier = pltpu.get_barrier_semaphore()

    def signal(k, unused):
        pl.semaphore_signal(
            barrier,
            inc=1,
            device_id=peer_at(lax.rem(me + k, count), tiles_y),
            device_id_type=MESH,
        )
        return unused

    lax.fori_loop(1, count, signal, 0)
    pl.semaphore_wait(barrier, count - 1)


def march(
    tiles_x,
    tiles_y,
    fields_ref,
    material_ref,
    eps_ref,
    loss_ref,
    wave_ref,
    final_ref,
    phasor_ref,
    e_ref,
    h_ref,
    keep_ref,
    curl_ref,
    row_out,
    row_e,
    row_h,
    col_out,
    col_e,
    col_h,
    row_g,
    col_g,
    row_d,
    col_d,
    row_far,
    col_far,
    phase,
    gathered,
    send_sem,
    recv_sem,
    gather_send,
    gather_recv,
):
    count = tiles_x * tiles_y
    depth, cells_x, cells_y = fields_ref.shape[1:]
    middle = depth // 2
    at_x = lax.axis_index("gx")
    at_y = lax.axis_index("gy")
    me = at_x * tiles_y + at_y
    tile = (cells_x, cells_y)
    row_id = lax.broadcasted_iota(jnp.int32, tile, 0)
    col_id = lax.broadcasted_iota(jnp.int32, tile, 1)
    last_row = row_id == cells_x - 1
    first_row = row_id == 0
    last_col = col_id == cells_y - 1
    first_col = col_id == 0
    blank = jnp.zeros(tile, jnp.float32)

    has_right_x = at_x < tiles_x - 1
    has_left_x = at_x > 0
    has_right_y = at_y < tiles_y - 1
    has_left_y = at_y > 0
    x_up, x_down = {"gx": at_x + 1}, {"gx": at_x - 1}
    y_up, y_down = {"gy": at_y + 1}, {"gy": at_y - 1}
    routes = (
        (row_out.at[0], row_e, x_down, has_left_x, has_right_x),
        (col_out.at[0], col_e, y_down, has_left_y, has_right_y),
        (row_far, row_g, x_up, has_right_x, has_left_x),
        (col_far, col_g, y_up, has_right_y, has_left_y),
        (
            row_far.at[2],
            row_d,
            {"gx": at_x + 1, "gy": at_y - 1},
            has_right_x & has_left_y,
            has_left_x & has_right_y,
        ),
        (
            col_far,
            col_d,
            {"gx": at_x - 1, "gy": at_y + 1},
            has_left_x & has_right_y,
            has_right_x & has_left_y,
        ),
        (row_out.at[1], row_h, x_up, has_right_x, has_left_x),
        (col_out.at[1], col_h, y_up, has_right_y, has_left_y),
    )

    def copy_of(slot, odd):
        source, target, device, _, _ = routes[slot]
        return pltpu.make_async_remote_copy(
            src_ref=source,
            dst_ref=target if slot > 5 else target.at[odd],
            send_sem=send_sem.at[slot],
            recv_sem=recv_sem.at[slot, odd],
            device_id=device,
            device_id_type=MESH,
        )

    def send(slot, odd):
        @pl.when(routes[slot][3])
        def _():
            copy_of(slot, odd).start()

    def sent(slot, odd):
        @pl.when(routes[slot][3])
        def _():
            copy_of(slot, odd).wait_send()

    def arrived(slot, odd):
        @pl.when(routes[slot][4])
        def _():
            copy_of(slot, odd).wait_recv()

    for halo in (row_e, row_h, col_e, col_h, row_g, col_g, row_d, col_d):
        halo[...] = jnp.zeros(halo.shape, jnp.float32)
    greet(me, count, tiles_y)

    keep_values = []
    curl_values = []
    for material in range(eps_ref.shape[0]):
        loss = jnp.full(tile, loss_ref[material], jnp.float32)
        eps = jnp.full(tile, eps_ref[material], jnp.float32)
        keep_values.append((1.0 - loss) / (1.0 + loss))
        curl_values.append(COURANT / (eps * (1.0 + loss)))
    for component in range(3):
        e_ref[component, depth] = blank
        h_ref[component, 0] = blank
    phase[...] = jnp.zeros(phase.shape, jnp.float32)

    def pack_columns(packed, z, first, second, column):
        packed = jnp.where(
            col_id == z, jnp.broadcast_to(first[:, column : column + 1], tile), packed
        )
        return jnp.where(
            col_id == depth + z,
            jnp.broadcast_to(second[:, column : column + 1], tile),
            packed,
        )

    def edges(z, ex, ey, ez, near, far):
        row_out[0, 0, pl.ds(z, 1), :] = ez[0:1]
        row_out[0, 1, pl.ds(z, 1), :] = ey[0:1]
        for place, values in enumerate((ez, ey, ex)):
            row_far[place, pl.ds(z, 1), :] = values[cells_x - 1 : cells_x]
        near = pack_columns(near, z, ez, ex, 0)
        far = pack_columns(far, z, ez, ex, cells_y - 1)
        far = jnp.where(
            col_id == 2 * depth + z,
            jnp.broadcast_to(ey[:, cells_y - 1 : cells_y], tile),
            far,
        )
        return near, far

    def load(block, packed):
        near, far, beyond = packed
        base = block * GROUP
        new = []
        for j in range(GROUP):
            materials = material_ref[base + j]
            keep = keep_values[0]
            curl = curl_values[0]
            for material in range(1, len(keep_values)):
                keep = jnp.where(materials == material, keep_values[material], keep)
                curl = jnp.where(materials == material, curl_values[material], curl)
            new.append((keep, curl, [fields_ref[c, base + j] for c in range(6)]))
        for j in range(GROUP):
            z = base + j
            keep_ref[z], curl_ref[z] = new[j][:2]
            values = new[j][2]
            for component in range(3):
                e_ref[component, z] = values[component]
                h_ref[component, z + 1] = values[3 + component]
            near, far = edges(z, values[0], values[1], values[2], near, far)
            row_out[1, 0, pl.ds(z, 1), :] = values[5][cells_x - 1 : cells_x]
            row_out[1, 1, pl.ds(z, 1), :] = values[4][cells_x - 1 : cells_x]
            beyond = pack_columns(beyond, z, values[5], values[3], cells_y - 1)
        return near, far, beyond

    col_out[0], col_far[...], col_out[1] = lax.fori_loop(
        0, depth // GROUP, load, (blank, blank, blank), unroll=True
    )
    for slot in range(8):
        send(slot, 0)
    for slot in (6, 7):
        arrived(slot, 0)

    plane = (depth, cells_y)
    depth_id = lax.broadcasted_iota(jnp.int32, plane, 0)
    plane_col = lax.broadcasted_iota(jnp.int32, plane, 1)
    keep_x = jnp.where(has_left_x, COURANT, 0.0)
    keep_y = jnp.where(has_left_y, COURANT, 0.0)

    def beyond_edges(odd):
        ez_g, ey_g, ex_g = row_g[odd, 0], row_g[odd, 1], row_g[odd, 2]
        ex_next = jnp.where(
            plane_col == cells_y - 1,
            pltpu.roll(row_d[odd], cells_y - 1, 1),
            pltpu.roll(ex_g, cells_y - 1, 1),
        )
        ex_up = jnp.where(depth_id == depth - 1, 0.0, pltpu.roll(ex_g, depth - 1, 0))
        row_h[0] = row_h[0] - keep_x * ((row_out[0, 1] - ey_g) - (ex_next - ex_g))
        row_h[1] = row_h[1] - keep_x * ((ex_up - ex_g) - (row_out[0, 0] - ez_g))

        near, far = col_out[0], col_g[odd]
        ahead = jnp.where(
            last_row, pltpu.roll(col_d[odd], cells_x - 1, 0), pltpu.roll(far, cells_x - 1, 0)
        )
        change = near - far
        dx_ey = pltpu.roll(ahead - far, cells_y - 2 * depth, 1)
        dy_ex = pltpu.roll(change, cells_y - depth, 1)
        up = jnp.where(col_id == 3 * depth - 1, 0.0, pltpu.roll(far, cells_y - 1, 1))
        dz_ey = pltpu.roll(up - far, cells_y - depth, 1)
        dy_ez = pltpu.roll(change, depth, 1)
        col_h[...] = col_h[...] - keep_y * jnp.where(
            col_id < depth, dx_ey - dy_ex, dy_ez - dz_ey
        )

    def step(turn, unused):
        odd = lax.rem(turn, 2)
        for slot in range(6):
            arrived(slot, odd)
        edge = col_e[odd]

        def magnetic(block, packed):
            base = block * GROUP
            ex = [e_ref[0, base + j] for j in range(GROUP + 1)]
            ey = [e_ref[1, base + j] for j in range(GROUP + 1)]
            ez = [e_ref[2, base + j] for j in range(GROUP)]
            new = []
            for j in range(GROUP):
                z = base + j
                row_z = jnp.broadcast_to(row_e[odd, 0, pl.ds(z, 1), :], tile)
                row_y = jnp.broadcast_to(row_e[odd, 1, pl.ds(z, 1), :], tile)
                col_z = pltpu.roll(edge, cells_y - 1 - z, 1)
                col_x = pltpu.roll(edge, cells_y - 1 - depth - z, 1)
                dx_ez = jnp.where(last_row, row_z, pltpu.roll(ez[j], cells_x - 1, 0)) - ez[j]
                dx_ey = jnp.where(last_row, row_y, pltpu.roll(ey[j], cells_x - 1, 0)) - ey[j]
                dy_ez = jnp.where(last_col, col_z, pltpu.roll(ez[j], cells_y - 1, 1)) - ez[j]
                dy_ex = jnp.where(last_col, col_x, pltpu.roll(ex[j], cells_y - 1, 1)) - ex[j]
                hx = h_ref[0, z + 1] - COURANT * (dy_ez - (ey[j + 1] - ey[j]))
                hy = h_ref[1, z + 1] - COURANT * ((ex[j + 1] - ex[j]) - dx_ez)
                hz = h_ref[2, z + 1] - COURANT * (dx_ey - dy_ex)
                new.append((hx, hy, hz))
            for j in range(GROUP):
                z = base + j
                hx, hy, hz = new[j]
                h_ref[0, z + 1] = hx
                h_ref[1, z + 1] = hy
                h_ref[2, z + 1] = hz
            return packed

        lax.fori_loop(0, depth // GROUP, magnetic, 0, unroll=True)
        beyond_edges(odd)
        for slot in range(6):
            sent(slot, odd)
        edge_h = col_h[...]

        def electric(block, packed):
            near, far = packed
            base = block * GROUP
            hx = [h_ref[0, base + j] for j in range(GROUP + 1)]
            hy = [h_ref[1, base + j] for j in range(GROUP + 1)]
            hz = [None] + [h_ref[2, base + j + 1] for j in range(GROUP)]
            new = []
            for j in range(1, GROUP + 1):
                z = base + j - 1
                row_z = jnp.broadcast_to(row_h[0, pl.ds(z, 1), :], tile)
                row_y = jnp.broadcast_to(row_h[1, pl.ds(z, 1), :], tile)
                col_z = pltpu.roll(edge_h, lax.rem(cells_y - z, cells_y), 1)
                col_x = pltpu.roll(edge_h, cells_y - depth - z, 1)
                dx_hz = hz[j] - jnp.where(first_row, row_z, pltpu.roll(hz[j], 1, 0))
                dx_hy = hy[j] - jnp.where(first_row, row_y, pltpu.roll(hy[j], 1, 0))
                dy_hz = hz[j] - jnp.where(first_col, col_z, pltpu.roll(hz[j], 1, 1))
                dy_hx = hx[j] - jnp.where(first_col, col_x, pltpu.roll(hx[j], 1, 1))
                keep, curl = keep_ref[z], curl_ref[z]
                ex = keep * e_ref[0, z] + curl * (dy_hz - (hy[j] - hy[j - 1]))
                ey = keep * e_ref[1, z] + curl * ((hx[j] - hx[j - 1]) - dx_hz)
                ez = keep * e_ref[2, z] + curl * (dx_hy - dy_hx)
                new.append((ex, ey, ez))
            for j in range(GROUP):
                z = base + j
                ex, ey, ez = new[j]
                e_ref[0, z] = ex
                e_ref[1, z] = ey
                e_ref[2, z] = ez
                near, far = edges(z, ex, ey, ez, near, far)
            return near, far

        col_out[0], col_far[...] = lax.fori_loop(
            0, depth // GROUP, electric, (blank, blank), unroll=True
        )

        @pl.when(turn < STEPS - 1)
        def _():
            for slot in range(6):
                send(slot, 1 - odd)

        for component in range(2):
            monitor = e_ref[component, middle]
            phase[component] = phase[component] + monitor * wave_ref[0, turn]
            phase[2 + component] = phase[2 + component] - monitor * wave_ref[1, turn]
        return unused

    lax.fori_loop(0, STEPS, step, 0)
    for slot in (6, 7):
        sent(slot, 0)

    def share(k):
        return pltpu.make_async_remote_copy(
            src_ref=phase,
            dst_ref=gathered.at[me],
            send_sem=gather_send.at[k],
            recv_sem=gather_recv.at[k],
            device_id=peer_at(lax.rem(me + k, count), tiles_y),
            device_id_type=MESH,
        )

    def start(k, unused):
        share(k).start()
        return unused

    lax.fori_loop(1, count, start, 0)

    def store(block, unused):
        base = block * GROUP
        values = [
            [e_ref[component, base + j] for component in range(3)]
            + [h_ref[component, base + j + 1] for component in range(3)]
            for j in range(GROUP)
        ]
        for j in range(GROUP):
            for component in range(6):
                final_ref[component, base + j] = values[j][component]
        return unused

    lax.fori_loop(0, depth // GROUP, store, 0, unroll=True)

    def finish(k, unused):
        share(k).wait_send()
        share(k).wait_recv()
        return unused

    lax.fori_loop(1, count, finish, 0)
    gathered[me] = phase[...]
    for tile_x in range(tiles_x):
        for tile_y in range(tiles_y):
            phasor_ref[
                :,
                tile_x * cells_x : (tile_x + 1) * cells_x,
                tile_y * cells_y : (tile_y + 1) * cells_y,
            ] = gathered[tile_x * tiles_y + tile_y]


def run_march(fields, material_map, material_eps, material_loss, tiles_x, tiles_y):
    depth, cells_x, cells_y = fields.shape[1:]
    count = tiles_x * tiles_y
    moments = np.float32(ANGULAR) * np.arange(1, STEPS + 1, dtype=np.float32)
    wave = jnp.asarray(np.stack((np.cos(moments), np.sin(moments))).astype(np.float32))
    vmem = pl.BlockSpec(memory_space=pltpu.VMEM)
    smem = pl.BlockSpec(memory_space=pltpu.SMEM)
    state = (3, depth + 1, cells_x, cells_y)
    return pl.pallas_call(
        functools.partial(march, tiles_x, tiles_y),
        out_shape=(
            jax.ShapeDtypeStruct(fields.shape, jnp.float32),
            jax.ShapeDtypeStruct((4, cells_x * tiles_x, cells_y * tiles_y), jnp.float32),
        ),
        in_specs=[vmem, vmem, smem, smem, smem],
        out_specs=(vmem, vmem),
        scratch_shapes=[
            pltpu.VMEM(state, jnp.float32),
            pltpu.VMEM(state, jnp.float32),
            pltpu.VMEM((depth, cells_x, cells_y), jnp.float32),
            pltpu.VMEM((depth, cells_x, cells_y), jnp.float32),
            pltpu.VMEM((2, 2, depth, cells_y), jnp.float32),
            pltpu.VMEM((2, 2, depth, cells_y), jnp.float32),
            pltpu.VMEM((2, depth, cells_y), jnp.float32),
            pltpu.VMEM((2, cells_x, cells_y), jnp.float32),
            pltpu.VMEM((2, cells_x, cells_y), jnp.float32),
            pltpu.VMEM((cells_x, cells_y), jnp.float32),
            pltpu.VMEM((2, 3, depth, cells_y), jnp.float32),
            pltpu.VMEM((2, cells_x, cells_y), jnp.float32),
            pltpu.VMEM((2, depth, cells_y), jnp.float32),
            pltpu.VMEM((2, cells_x, cells_y), jnp.float32),
            pltpu.VMEM((3, depth, cells_y), jnp.float32),
            pltpu.VMEM((cells_x, cells_y), jnp.float32),
            pltpu.VMEM((4, cells_x, cells_y), jnp.float32),
            pltpu.VMEM((count, 4, cells_x, cells_y), jnp.float32),
            pltpu.SemaphoreType.DMA((8,)),
            pltpu.SemaphoreType.DMA((8, 2)),
            pltpu.SemaphoreType.DMA((count,)),
            pltpu.SemaphoreType.DMA((count,)),
        ],
        compiler_params=pltpu.CompilerParams(
            collective_id=0, has_side_effects=True, vmem_limit_bytes=40 * 1024 * 1024
        ),
    )(fields, material_map, material_eps, material_loss, wave)


def picture(
    tiles_x,
    tiles_y,
    orders_ref,
    shift_ref,
    mask_ref,
    weight_ref,
    rows_ref,
    g_ref,
    image_ref,
    columns,
    part,
    swapped,
    crossed,
    strips,
    landed,
    swap_send,
    swap_recv,
    cross_send,
    cross_recv,
    hand_send,
    hand_recv,
):
    count = tiles_x * tiles_y
    me = lax.axis_index("gx") * tiles_y + lax.axis_index("gy")
    sources = mask_ref.shape[0]
    size_p = mask_ref.shape[1] // 2
    size_q = mask_ref.shape[2] // 2
    pixels = image_ref.shape[1]
    strip = image_ref.shape[0]
    greet(me, count, tiles_y)

    def one_hot(size, offset, flipped):
        to_id = lax.broadcasted_iota(jnp.int32, (2 * size, 2 * size), 1 if flipped else 0)
        from_id = lax.broadcasted_iota(jnp.int32, (2 * size, 2 * size), 0 if flipped else 1)
        to_half = jnp.where(to_id >= size, size, 0)
        moved = to_id - to_half + offset
        moved = jnp.where(moved < 0, moved + size, moved)
        moved = jnp.where(moved >= size, moved - size, moved)
        return jnp.where(from_id == moved + to_half, 1.0, 0.0).astype(jnp.bfloat16)

    def prepare(source, unused):
        pick_p = one_hot(size_p, shift_ref[source, 0], False)
        pick_q = one_hot(size_q, shift_ref[source, 1], True)
        rolled = jnp.dot(pick_p, orders_ref[...], preferred_element_type=jnp.float32)
        rolled = jnp.dot(
            rolled.astype(jnp.bfloat16), pick_q, preferred_element_type=jnp.float32
        )
        masked = (rolled * mask_ref[source].astype(jnp.float32)).astype(jnp.bfloat16)
        spread = jnp.dot(masked, g_ref[...], preferred_element_type=jnp.float32)
        spread = spread.astype(jnp.bfloat16)
        for block in range(2):
            real = spread[block * size_p : (block + 1) * size_p, :pixels]
            imag = spread[block * size_p : (block + 1) * size_p, pixels:]
            at = 2 * block * pixels
            columns[source, :size_p, at : at + pixels] = real
            columns[source, :size_p, at + pixels : at + 2 * pixels] = imag
            columns[source, size_p:, at : at + pixels] = -imag
            columns[source, size_p:, at + pixels : at + 2 * pixels] = real
        return unused

    lax.fori_loop(0, sources, prepare, 0)

    pairs = tiles_x // 2
    at_x = lax.axis_index("gx")
    at_y = lax.axis_index("gy")
    core = lax.rem(at_x, 2)
    at_pair = at_x // 2
    scale = 1.0 / (sources * count)
    high = tiles_y * strip

    def render(pair, half):
        table = rows_ref[
            pl.ds(pl.multiple_of((2 * pair + half) * high, high), high), :
        ]
        total = jnp.zeros((high, pixels), jnp.float32)
        for source in range(sources):
            bright = None
            for block in range(4):
                values = jnp.dot(
                    table,
                    columns[source, :, block * pixels : (block + 1) * pixels],
                    preferred_element_type=jnp.float32,
                )
                squared = values * values
                bright = squared if bright is None else bright + squared
            total = total + (weight_ref[source] * scale) * bright
        part[pair, half] = total

    def swap(pair):
        return pltpu.make_async_remote_copy(
            src_ref=part.at[pair, 1 - core],
            dst_ref=swapped.at[pair],
            send_sem=swap_send.at[pair],
            recv_sem=swap_recv.at[pair],
            device_id={"gx": at_x + 1 - 2 * core},
            device_id_type=MESH,
        )

    def cross(k):
        pair = lax.rem(at_pair + k, pairs)
        return pltpu.make_async_remote_copy(
            src_ref=part.at[pair, core],
            dst_ref=crossed.at[k],
            send_sem=cross_send.at[k],
            recv_sem=cross_recv.at[k],
            device_id={"gx": 2 * pair + core},
            device_id_type=MESH,
        )

    def away(k):
        return lax.rem(at_pair + k, pairs)

    def first(turn, unused):
        pair = away(turn + 1)
        render(pair, 1 - core)
        swap(pair).start()
        render(pair, core)
        return unused

    lax.fori_loop(0, pairs, first, 0)

    def second(turn, unused):
        pair = away(turn + 1)
        swap(pair).wait_recv()
        part[pair, core] = part[pair, core] + swapped[pair]

        @pl.when(turn < pairs - 1)
        def _():
            cross(turn + 1).start()

        return unused

    lax.fori_loop(0, pairs, second, 0)

    def gather_pairs(k, running):
        cross(k).wait_recv()
        return running + crossed[k]

    mine = lax.fori_loop(1, pairs, gather_pairs, part[at_pair, core])
    for owner in range(tiles_y):
        strips[owner] = mine[owner * strip : (owner + 1) * strip]

    def hand(k):
        owner = lax.rem(at_y + k, tiles_y)
        return pltpu.make_async_remote_copy(
            src_ref=strips.at[owner],
            dst_ref=landed.at[k],
            send_sem=hand_send.at[k],
            recv_sem=hand_recv.at[k],
            device_id={"gy": owner},
            device_id_type=MESH,
        )

    for k in range(1, tiles_y):
        hand(k).start()
    total = strips[at_y]
    for k in range(1, tiles_y):
        hand(k).wait_recv()
        total = total + landed[k]
    image_ref[...] = total
    for k in range(1, tiles_y):
        hand(k).wait_send()

    def finish(pair, unused):
        swap(pair).wait_send()

        @pl.when(pair > 0)
        def _():
            cross(pair).wait_send()

        return unused

    lax.fori_loop(0, pairs, finish, 0)


def run_picture(orders, shift, mask, weight, row_table, g_matrix, tiles_x, tiles_y):
    count = tiles_x * tiles_y
    pixels = row_table.shape[0]
    strip = pixels // count
    pairs = tiles_x // 2
    vmem = pl.BlockSpec(memory_space=pltpu.VMEM)
    smem = pl.BlockSpec(memory_space=pltpu.SMEM)
    return pl.pallas_call(
        functools.partial(picture, tiles_x, tiles_y),
        out_shape=jax.ShapeDtypeStruct((strip, pixels), jnp.float32),
        in_specs=[vmem, smem, vmem, smem, vmem, vmem],
        out_specs=vmem,
        scratch_shapes=[
            pltpu.VMEM((mask.shape[0], row_table.shape[1], 4 * pixels), jnp.bfloat16),
            pltpu.VMEM((pairs, 2, tiles_y * strip, pixels), jnp.float32),
            pltpu.VMEM((pairs, tiles_y * strip, pixels), jnp.float32),
            pltpu.VMEM((pairs, tiles_y * strip, pixels), jnp.float32),
            pltpu.VMEM((tiles_y, strip, pixels), jnp.float32),
            pltpu.VMEM((tiles_y, strip, pixels), jnp.float32),
        ]
        + [pltpu.SemaphoreType.DMA((pairs,))] * 4
        + [pltpu.SemaphoreType.DMA((tiles_y,))] * 2,
        compiler_params=pltpu.CompilerParams(
            collective_id=1, has_side_effects=True, vmem_limit_bytes=48 * 1024 * 1024
        ),
    )(orders, shift, mask, weight, row_table, g_matrix)


def spectrum(extent, orders, period):
    wrapped = ((np.arange(orders) - orders // 2)[:, None] * np.arange(extent)[None, :]) % period
    angles = 2.0 * math.pi / period * wrapped
    return np.cos(angles).astype(np.float32), np.sin(angles).astype(np.float32)


def image_tables(pixels, orders_p, orders_q):
    cos_u, sin_u = spectrum(pixels, orders_p, pixels)
    row_table = np.concatenate((cos_u.T, sin_u.T), 1) * np.float32(1.0 / math.sqrt(orders_p))
    cos_v, sin_v = spectrum(pixels, orders_q, pixels)
    real_v = cos_v * np.float32(1.0 / math.sqrt(orders_q))
    imag_v = sin_v * np.float32(1.0 / math.sqrt(orders_q))
    g_matrix = np.block([[real_v, imag_v], [-imag_v, real_v]])
    return (row_table.astype(jnp.bfloat16), g_matrix.astype(jnp.bfloat16))


def body(
    fields, material_map, material_eps, material_loss, source_shift, source_mask, source_weight
):
    tiles_x = lax.axis_size("gx")
    tiles_y = lax.axis_size("gy")
    orders_p, orders_q = source_mask.shape[1:]
    final_fields, phasor = run_march(
        fields, material_map, material_eps, material_loss, tiles_x, tiles_y
    )
    period_x, period_y = phasor.shape[1:]
    cos_x, sin_x = spectrum(period_x, orders_p, period_x)
    cos_y, sin_y = spectrum(period_y, orders_q, period_y)
    both_y = jnp.asarray(np.concatenate((cos_y, sin_y), 0).T)
    along = jnp.dot(
        phasor.reshape(4 * period_x, period_y), both_y, precision=PRECISE
    ).reshape(2, 2, period_x, 2 * orders_q)
    part_re = along[0, :, :, :orders_q] + along[1, :, :, orders_q:]
    part_im = along[1, :, :, :orders_q] - along[0, :, :, orders_q:]
    both_x = jnp.asarray(np.concatenate((cos_x, sin_x), 1))
    stacked = jnp.concatenate(
        (
            jnp.concatenate((part_re, part_im), 2),
            jnp.concatenate((part_im, -part_re), 2),
        ),
        1,
    )
    orders = jnp.einsum("px,cxq->cpq", both_x, stacked, precision=PRECISE)
    scaling = 1.0 / math.sqrt(period_x * period_y * STEPS)
    orders_b = (orders * scaling).astype(jnp.bfloat16).reshape(2 * orders_p, 2 * orders_q)
    row_table, g_matrix = image_tables(M, orders_p, orders_q)
    mask = jnp.tile(source_mask.astype(jnp.bfloat16), (1, 2, 2))
    image = run_picture(
        orders_b,
        source_shift,
        mask,
        source_weight,
        jnp.asarray(row_table),
        jnp.asarray(g_matrix),
        tiles_x,
        tiles_y,
    )
    return (final_fields, image)


def solution(mesh):
    placed = (
        P("clips", None, "gx", "gy"),
        P("clips", "gx", "gy"),
        P(),
        P(),
        P(("gx", "gy"), None),
        P(("gx", "gy"), None, None),
        P(("gx", "gy")),
    )
    return jax.shard_map(
        body,
        mesh=mesh,
        in_specs=placed,
        out_specs=(P("clips", None, "gx", "gy"), P(("gx", "gy"), "clips")),
        check_vma=False,
    )
```

```python
import functools
import math

import jax
import jax.numpy as jnp
import numpy as np
from jax import lax
from jax.experimental import pallas as pl
from jax.experimental.pallas import tpu as pltpu
from jax.sharding import PartitionSpec as P

STEPS = 12
M = 512
COURANT = 0.55
ANGULAR = 0.7
PRECISE = lax.Precision.HIGHEST
MESH = pl.DeviceIdType.MESH
GROUP = 16


def peer_at(index, tiles_y):
    return {"gx": index // tiles_y, "gy": lax.rem(index, tiles_y)}


def greet(me, count, tiles_y):
    barrier = pltpu.get_barrier_semaphore()

    def signal(k, unused):
        pl.semaphore_signal(
            barrier,
            inc=1,
            device_id=peer_at(lax.rem(me + k, count), tiles_y),
            device_id_type=MESH,
        )
        return unused

    lax.fori_loop(1, count, signal, 0)
    pl.semaphore_wait(barrier, count - 1)


def march(
    tiles_x,
    tiles_y,
    fields_ref,
    material_ref,
    eps_ref,
    loss_ref,
    final_ref,
    phasor_ref,
    e_ref,
    h_ref,
    keep_ref,
    curl_ref,
    row_out,
    row_e,
    row_h,
    col_out,
    col_e,
    col_h,
    row_g,
    col_g,
    row_d,
    col_d,
    row_far,
    col_far,
    phase,
    gathered,
    send_sem,
    recv_sem,
    gather_send,
    gather_recv,
    wave_ref,
):
    count = tiles_x * tiles_y
    depth, cells_x, cells_y = fields_ref.shape[1:]
    middle = depth // 2
    at_x = lax.axis_index("gx")
    at_y = lax.axis_index("gy")
    me = at_x * tiles_y + at_y
    tile = (cells_x, cells_y)
    row_id = lax.broadcasted_iota(jnp.int32, tile, 0)
    col_id = lax.broadcasted_iota(jnp.int32, tile, 1)
    last_row = row_id == cells_x - 1
    first_row = row_id == 0
    last_col = col_id == cells_y - 1
    first_col = col_id == 0
    blank = jnp.zeros(tile, jnp.float32)
    for turn in range(STEPS):
        moment = float(np.float32(ANGULAR) * np.float32(turn + 1))
        wave_ref[0, turn] = math.cos(moment)
        wave_ref[1, turn] = math.sin(moment)

    has_right_x = at_x < tiles_x - 1
    has_left_x = at_x > 0
    has_right_y = at_y < tiles_y - 1
    has_left_y = at_y > 0
    x_up, x_down = {"gx": at_x + 1}, {"gx": at_x - 1}
    y_up, y_down = {"gy": at_y + 1}, {"gy": at_y - 1}
    routes = (
        (row_out.at[0], row_e, x_down, has_left_x, has_right_x),
        (col_out.at[0], col_e, y_down, has_left_y, has_right_y),
        (row_far, row_g, x_up, has_right_x, has_left_x),
        (col_far, col_g, y_up, has_right_y, has_left_y),
        (
            row_far.at[2],
            row_d,
            {"gx": at_x + 1, "gy": at_y - 1},
            has_right_x & has_left_y,
            has_left_x & has_right_y,
        ),
        (
            col_far,
            col_d,
            {"gx": at_x - 1, "gy": at_y + 1},
            has_left_x & has_right_y,
            has_right_x & has_left_y,
        ),
        (row_out.at[1], row_h, x_up, has_right_x, has_left_x),
        (col_out.at[1], col_h, y_up, has_right_y, has_left_y),
    )

    def copy_of(slot, odd):
        source, target, device, _, _ = routes[slot]
        return pltpu.make_async_remote_copy(
            src_ref=source,
            dst_ref=target if slot > 5 else target.at[odd],
            send_sem=send_sem.at[slot],
            recv_sem=recv_sem.at[slot, odd],
            device_id=device,
            device_id_type=MESH,
        )

    def send(slot, odd):
        @pl.when(routes[slot][3])
        def _():
            copy_of(slot, odd).start()

    def sent(slot, odd):
        @pl.when(routes[slot][3])
        def _():
            copy_of(slot, odd).wait_send()

    def arrived(slot, odd):
        @pl.when(routes[slot][4])
        def _():
            copy_of(slot, odd).wait_recv()

    for halo in (row_e, row_h, col_e, col_h, row_g, col_g, row_d, col_d):
        halo[...] = jnp.zeros(halo.shape, jnp.float32)
    greet(me, count, tiles_y)

    keep_values = []
    curl_values = []
    for material in range(eps_ref.shape[0]):
        loss = jnp.full(tile, loss_ref[material], jnp.float32)
        eps = jnp.full(tile, eps_ref[material], jnp.float32)
        keep_values.append((1.0 - loss) / (1.0 + loss))
        curl_values.append(COURANT / (eps * (1.0 + loss)))
    for component in range(3):
        e_ref[component, depth] = blank
        h_ref[component, 0] = blank
    phase[...] = jnp.zeros(phase.shape, jnp.float32)

    def pack_columns(packed, z, first, second, column):
        packed = jnp.where(
            col_id == z, jnp.broadcast_to(first[:, column : column + 1], tile), packed
        )
        return jnp.where(
            col_id == depth + z,
            jnp.broadcast_to(second[:, column : column + 1], tile),
            packed,
        )

    def edges(z, ex, ey, ez, near, far):
        row_out[0, 0, pl.ds(z, 1), :] = ez[0:1]
        row_out[0, 1, pl.ds(z, 1), :] = ey[0:1]
        for place, values in enumerate((ez, ey, ex)):
            row_far[place, pl.ds(z, 1), :] = values[cells_x - 1 : cells_x]
        near = pack_columns(near, z, ez, ex, 0)
        far = pack_columns(far, z, ez, ex, cells_y - 1)
        far = jnp.where(
            col_id == 2 * depth + z,
            jnp.broadcast_to(ey[:, cells_y - 1 : cells_y], tile),
            far,
        )
        return near, far

    def load(block, packed):
        near, far, beyond = packed
        base = block * GROUP
        new = []
        for j in range(GROUP):
            materials = material_ref[base + j]
            keep = keep_values[0]
            curl = curl_values[0]
            for material in range(1, len(keep_values)):
                keep = jnp.where(materials == material, keep_values[material], keep)
                curl = jnp.where(materials == material, curl_values[material], curl)
            new.append((keep, curl, [fields_ref[c, base + j] for c in range(6)]))
        for j in range(GROUP):
            z = base + j
            keep_ref[z], curl_ref[z] = new[j][:2]
            values = new[j][2]
            for component in range(3):
                e_ref[component, z] = values[component]
                h_ref[component, z + 1] = values[3 + component]
            near, far = edges(z, values[0], values[1], values[2], near, far)
            row_out[1, 0, pl.ds(z, 1), :] = values[5][cells_x - 1 : cells_x]
            row_out[1, 1, pl.ds(z, 1), :] = values[4][cells_x - 1 : cells_x]
            beyond = pack_columns(beyond, z, values[5], values[3], cells_y - 1)
        return near, far, beyond

    col_out[0], col_far[...], col_out[1] = lax.fori_loop(
        0, depth // GROUP, load, (blank, blank, blank), unroll=True
    )
    for slot in range(8):
        send(slot, 0)
    for slot in (6, 7):
        arrived(slot, 0)

    plane = (depth, cells_y)
    depth_id = lax.broadcasted_iota(jnp.int32, plane, 0)
    plane_col = lax.broadcasted_iota(jnp.int32, plane, 1)
    keep_x = jnp.where(has_left_x, COURANT, 0.0)
    keep_y = jnp.where(has_left_y, COURANT, 0.0)

    def beyond_edges(odd):
        ez_g, ey_g, ex_g = row_g[odd, 0], row_g[odd, 1], row_g[odd, 2]
        ex_next = jnp.where(
            plane_col == cells_y - 1,
            pltpu.roll(row_d[odd], cells_y - 1, 1),
            pltpu.roll(ex_g, cells_y - 1, 1),
        )
        ex_up = jnp.where(depth_id == depth - 1, 0.0, pltpu.roll(ex_g, depth - 1, 0))
        row_h[0] = row_h[0] - keep_x * ((row_out[0, 1] - ey_g) - (ex_next - ex_g))
        row_h[1] = row_h[1] - keep_x * ((ex_up - ex_g) - (row_out[0, 0] - ez_g))

        near, far = col_out[0], col_g[odd]
        ahead = jnp.where(
            last_row, pltpu.roll(col_d[odd], cells_x - 1, 0), pltpu.roll(far, cells_x - 1, 0)
        )
        change = near - far
        dx_ey = pltpu.roll(ahead - far, cells_y - 2 * depth, 1)
        dy_ex = pltpu.roll(change, cells_y - depth, 1)
        up = jnp.where(col_id == 3 * depth - 1, 0.0, pltpu.roll(far, cells_y - 1, 1))
        dz_ey = pltpu.roll(up - far, cells_y - depth, 1)
        dy_ez = pltpu.roll(change, depth, 1)
        col_h[...] = col_h[...] - keep_y * jnp.where(
            col_id < depth, dx_ey - dy_ex, dy_ez - dz_ey
        )

    def step(turn, unused):
        odd = lax.rem(turn, 2)
        for slot in (0, 1):
            arrived(slot, odd)
        edge = col_e[odd]

        def magnetic(block, packed):
            base = block * GROUP
            ex = [e_ref[0, base + j] for j in range(GROUP + 1)]
            ey = [e_ref[1, base + j] for j in range(GROUP + 1)]
            ez = [e_ref[2, base + j] for j in range(GROUP)]
            new = []
            for j in range(GROUP):
                z = base + j
                row_z = jnp.broadcast_to(row_e[odd, 0, pl.ds(z, 1), :], tile)
                row_y = jnp.broadcast_to(row_e[odd, 1, pl.ds(z, 1), :], tile)
                col_z = pltpu.roll(edge, cells_y - 1 - z, 1)
                col_x = pltpu.roll(edge, cells_y - 1 - depth - z, 1)
                dx_ez = jnp.where(last_row, row_z, pltpu.roll(ez[j], cells_x - 1, 0)) - ez[j]
                dx_ey = jnp.where(last_row, row_y, pltpu.roll(ey[j], cells_x - 1, 0)) - ey[j]
                dy_ez = jnp.where(last_col, col_z, pltpu.roll(ez[j], cells_y - 1, 1)) - ez[j]
                dy_ex = jnp.where(last_col, col_x, pltpu.roll(ex[j], cells_y - 1, 1)) - ex[j]
                hx = h_ref[0, z + 1] - COURANT * (dy_ez - (ey[j + 1] - ey[j]))
                hy = h_ref[1, z + 1] - COURANT * ((ex[j + 1] - ex[j]) - dx_ez)
                hz = h_ref[2, z + 1] - COURANT * (dx_ey - dy_ex)
                new.append((hx, hy, hz))
            for j in range(GROUP):
                z = base + j
                hx, hy, hz = new[j]
                h_ref[0, z + 1] = hx
                h_ref[1, z + 1] = hy
                h_ref[2, z + 1] = hz
            return packed

        lax.fori_loop(0, depth // GROUP, magnetic, 0, unroll=True)
        for slot in (2, 3, 4, 5):
            arrived(slot, odd)
        beyond_edges(odd)
        for slot in range(6):
            sent(slot, odd)
        edge_h = col_h[...]

        def electric(block, packed):
            near, far = packed
            base = block * GROUP
            hx = [h_ref[0, base + j] for j in range(GROUP + 1)]
            hy = [h_ref[1, base + j] for j in range(GROUP + 1)]
            hz = [None] + [h_ref[2, base + j + 1] for j in range(GROUP)]
            new = []
            for j in range(1, GROUP + 1):
                z = base + j - 1
                row_z = jnp.broadcast_to(row_h[0, pl.ds(z, 1), :], tile)
                row_y = jnp.broadcast_to(row_h[1, pl.ds(z, 1), :], tile)
                col_z = pltpu.roll(edge_h, lax.rem(cells_y - z, cells_y), 1)
                col_x = pltpu.roll(edge_h, cells_y - depth - z, 1)
                dx_hz = hz[j] - jnp.where(first_row, row_z, pltpu.roll(hz[j], 1, 0))
                dx_hy = hy[j] - jnp.where(first_row, row_y, pltpu.roll(hy[j], 1, 0))
                dy_hz = hz[j] - jnp.where(first_col, col_z, pltpu.roll(hz[j], 1, 1))
                dy_hx = hx[j] - jnp.where(first_col, col_x, pltpu.roll(hx[j], 1, 1))
                keep, curl = keep_ref[z], curl_ref[z]
                ex = keep * e_ref[0, z] + curl * (dy_hz - (hy[j] - hy[j - 1]))
                ey = keep * e_ref[1, z] + curl * ((hx[j] - hx[j - 1]) - dx_hz)
                ez = keep * e_ref[2, z] + curl * (dx_hy - dy_hx)
                new.append((ex, ey, ez))
            for j in range(GROUP):
                z = base + j
                ex, ey, ez = new[j]
                e_ref[0, z] = ex
                e_ref[1, z] = ey
                e_ref[2, z] = ez
                near, far = edges(z, ex, ey, ez, near, far)
            return near, far

        col_out[0], col_far[...] = lax.fori_loop(
            0, depth // GROUP, electric, (blank, blank), unroll=True
        )

        @pl.when(turn < STEPS - 1)
        def _():
            for slot in (0, 1, 4, 5, 2, 3):
                send(slot, 1 - odd)

        for component in range(2):
            monitor = e_ref[component, middle]
            phase[component] = phase[component] + monitor * wave_ref[0, turn]
            phase[2 + component] = phase[2 + component] - monitor * wave_ref[1, turn]
        return unused

    lax.fori_loop(0, STEPS, step, 0)
    for slot in (6, 7):
        sent(slot, 0)

    def share(k):
        return pltpu.make_async_remote_copy(
            src_ref=phase,
            dst_ref=gathered.at[me],
            send_sem=gather_send.at[k],
            recv_sem=gather_recv.at[k],
            device_id=peer_at(lax.rem(me + k, count), tiles_y),
            device_id_type=MESH,
        )

    def start(k, unused):
        share(k).start()
        return unused

    lax.fori_loop(1, count, start, 0)

    def store(block, unused):
        base = block * GROUP
        values = [
            [e_ref[component, base + j] for component in range(3)]
            + [h_ref[component, base + j + 1] for component in range(3)]
            for j in range(GROUP)
        ]
        for j in range(GROUP):
            for component in range(6):
                final_ref[component, base + j] = values[j][component]
        return unused

    lax.fori_loop(0, depth // GROUP, store, 0, unroll=True)

    def finish(k, unused):
        share(k).wait_send()
        share(k).wait_recv()
        return unused

    lax.fori_loop(1, count, finish, 0)
    gathered[me] = phase[...]
    for tile_x in range(tiles_x):
        for tile_y in range(tiles_y):
            phasor_ref[
                :,
                tile_x * cells_x : (tile_x + 1) * cells_x,
                tile_y * cells_y : (tile_y + 1) * cells_y,
            ] = gathered[tile_x * tiles_y + tile_y]


def run_march(fields, material_map, material_eps, material_loss, tiles_x, tiles_y):
    depth, cells_x, cells_y = fields.shape[1:]
    count = tiles_x * tiles_y
    vmem = pl.BlockSpec(memory_space=pltpu.VMEM)
    smem = pl.BlockSpec(memory_space=pltpu.SMEM)
    state = (3, depth + 1, cells_x, cells_y)
    return pl.pallas_call(
        functools.partial(march, tiles_x, tiles_y),
        out_shape=(
            jax.ShapeDtypeStruct(fields.shape, jnp.float32),
            jax.ShapeDtypeStruct((4, cells_x * tiles_x, cells_y * tiles_y), jnp.float32),
        ),
        in_specs=[vmem, vmem, smem, smem],
        out_specs=(vmem, vmem),
        scratch_shapes=[
            pltpu.VMEM(state, jnp.float32),
            pltpu.VMEM(state, jnp.float32),
            pltpu.VMEM((depth, cells_x, cells_y), jnp.float32),
            pltpu.VMEM((depth, cells_x, cells_y), jnp.float32),
            pltpu.VMEM((2, 2, depth, cells_y), jnp.float32),
            pltpu.VMEM((2, 2, depth, cells_y), jnp.float32),
            pltpu.VMEM((2, depth, cells_y), jnp.float32),
            pltpu.VMEM((2, cells_x, cells_y), jnp.float32),
            pltpu.VMEM((2, cells_x, cells_y), jnp.float32),
            pltpu.VMEM((cells_x, cells_y), jnp.float32),
            pltpu.VMEM((2, 3, depth, cells_y), jnp.float32),
            pltpu.VMEM((2, cells_x, cells_y), jnp.float32),
            pltpu.VMEM((2, depth, cells_y), jnp.float32),
            pltpu.VMEM((2, cells_x, cells_y), jnp.float32),
            pltpu.VMEM((3, depth, cells_y), jnp.float32),
            pltpu.VMEM((cells_x, cells_y), jnp.float32),
            pltpu.VMEM((4, cells_x, cells_y), jnp.float32),
            pltpu.VMEM((count, 4, cells_x, cells_y), jnp.float32),
            pltpu.SemaphoreType.DMA((8,)),
            pltpu.SemaphoreType.DMA((8, 2)),
            pltpu.SemaphoreType.DMA((count,)),
            pltpu.SemaphoreType.DMA((count,)),
            pltpu.SMEM((2, STEPS), jnp.float32),
        ],
        compiler_params=pltpu.CompilerParams(
            collective_id=0, has_side_effects=True, vmem_limit_bytes=40 * 1024 * 1024
        ),
    )(fields, material_map, material_eps, material_loss)


def picture(
    tiles_x,
    tiles_y,
    orders_ref,
    shift_ref,
    mask_ref,
    weight_ref,
    rows_ref,
    g_ref,
    image_ref,
    columns,
    part,
    swapped,
    crossed,
    strips,
    landed,
    swap_send,
    swap_recv,
    cross_send,
    cross_recv,
    hand_send,
    hand_recv,
):
    count = tiles_x * tiles_y
    me = lax.axis_index("gx") * tiles_y + lax.axis_index("gy")
    sources = mask_ref.shape[0]
    size_p, size_q = mask_ref.shape[1:]
    pixels = image_ref.shape[1]
    strip = image_ref.shape[0]
    greet(me, count, tiles_y)

    def one_hot(size, offset, flipped):
        to_id = lax.broadcasted_iota(jnp.int32, (2 * size, 2 * size), 1 if flipped else 0)
        from_id = lax.broadcasted_iota(jnp.int32, (2 * size, 2 * size), 0 if flipped else 1)
        to_half = jnp.where(to_id >= size, size, 0)
        moved = to_id - to_half + offset
        moved = jnp.where(moved < 0, moved + size, moved)
        moved = jnp.where(moved >= size, moved - size, moved)
        return jnp.where(from_id == moved + to_half, 1.0, 0.0).astype(jnp.bfloat16)

    def prepare(source, unused):
        pick_p = one_hot(size_p, shift_ref[source, 0], False)
        pick_q = one_hot(size_q, shift_ref[source, 1], True)
        rolled = jnp.dot(pick_p, orders_ref[...], preferred_element_type=jnp.float32)
        rolled = jnp.dot(
            rolled.astype(jnp.bfloat16), pick_q, preferred_element_type=jnp.float32
        )
        passed = mask_ref[source].astype(jnp.float32)
        passed = jnp.concatenate((passed, passed), 1)
        passed = jnp.concatenate((passed, passed), 0)
        masked = (rolled * passed).astype(jnp.bfloat16)
        spread = jnp.dot(masked, g_ref[...], preferred_element_type=jnp.float32)
        spread = spread.astype(jnp.bfloat16)
        for block in range(2):
            real = spread[block * size_p : (block + 1) * size_p, :pixels]
            imag = spread[block * size_p : (block + 1) * size_p, pixels:]
            at = 2 * block * pixels
            columns[source, :size_p, at : at + pixels] = real
            columns[source, :size_p, at + pixels : at + 2 * pixels] = imag
            columns[source, size_p:, at : at + pixels] = -imag
            columns[source, size_p:, at + pixels : at + 2 * pixels] = real
        return unused

    lax.fori_loop(0, sources, prepare, 0)

    pairs = tiles_x // 2
    at_x = lax.axis_index("gx")
    at_y = lax.axis_index("gy")
    core = lax.rem(at_x, 2)
    at_pair = at_x // 2
    scale = 1.0 / (sources * count)
    high = tiles_y * strip

    def render(pair, half):
        table = rows_ref[
            pl.ds(pl.multiple_of((2 * pair + half) * high, high), high), :
        ]
        total = jnp.zeros((high, pixels), jnp.float32)
        for source in range(sources):
            bright = None
            for block in range(4):
                values = jnp.dot(
                    table,
                    columns[source, :, block * pixels : (block + 1) * pixels],
                    preferred_element_type=jnp.float32,
                )
                squared = values * values
                bright = squared if bright is None else bright + squared
            total = total + (weight_ref[source] * scale) * bright
        part[pair, half] = total

    def swap(pair):
        return pltpu.make_async_remote_copy(
            src_ref=part.at[pair, 1 - core],
            dst_ref=swapped.at[pair],
            send_sem=swap_send.at[pair],
            recv_sem=swap_recv.at[pair],
            device_id={"gx": at_x + 1 - 2 * core},
            device_id_type=MESH,
        )

    def cross(k):
        pair = lax.rem(at_pair + k, pairs)
        return pltpu.make_async_remote_copy(
            src_ref=part.at[pair, core],
            dst_ref=crossed.at[k],
            send_sem=cross_send.at[k],
            recv_sem=cross_recv.at[k],
            device_id={"gx": 2 * pair + core},
            device_id_type=MESH,
        )

    def away(k):
        return lax.rem(at_pair + k, pairs)

    def first(turn, unused):
        pair = away(turn + 1)
        render(pair, 1 - core)
        swap(pair).start()
        render(pair, core)
        return unused

    lax.fori_loop(0, pairs, first, 0)

    def second(turn, unused):
        pair = away(turn + 1)
        swap(pair).wait_recv()
        part[pair, core] = part[pair, core] + swapped[pair]

        @pl.when(turn < pairs - 1)
        def _():
            cross(turn + 1).start()

        return unused

    lax.fori_loop(0, pairs, second, 0)

    def gather_pairs(k, running):
        cross(k).wait_recv()
        return running + crossed[k]

    mine = lax.fori_loop(1, pairs, gather_pairs, part[at_pair, core])
    for owner in range(tiles_y):
        strips[owner] = mine[owner * strip : (owner + 1) * strip]

    def hand(k):
        owner = lax.rem(at_y + k, tiles_y)
        return pltpu.make_async_remote_copy(
            src_ref=strips.at[owner],
            dst_ref=landed.at[k],
            send_sem=hand_send.at[k],
            recv_sem=hand_recv.at[k],
            device_id={"gy": owner},
            device_id_type=MESH,
        )

    for k in range(1, tiles_y):
        hand(k).start()
    total = strips[at_y]
    for k in range(1, tiles_y):
        hand(k).wait_recv()
        total = total + landed[k]
    image_ref[...] = total
    for k in range(1, tiles_y):
        hand(k).wait_send()

    def finish(pair, unused):
        swap(pair).wait_send()

        @pl.when(pair > 0)
        def _():
            cross(pair).wait_send()

        return unused

    lax.fori_loop(0, pairs, finish, 0)


def run_picture(orders, shift, mask, weight, row_table, g_matrix, tiles_x, tiles_y):
    count = tiles_x * tiles_y
    pixels = row_table.shape[0]
    strip = pixels // count
    pairs = tiles_x // 2
    vmem = pl.BlockSpec(memory_space=pltpu.VMEM)
    smem = pl.BlockSpec(memory_space=pltpu.SMEM)
    return pl.pallas_call(
        functools.partial(picture, tiles_x, tiles_y),
        out_shape=jax.ShapeDtypeStruct((strip, pixels), jnp.float32),
        in_specs=[vmem, smem, vmem, smem, vmem, vmem],
        out_specs=vmem,
        scratch_shapes=[
            pltpu.VMEM((mask.shape[0], row_table.shape[1], 4 * pixels), jnp.bfloat16),
            pltpu.VMEM((pairs, 2, tiles_y * strip, pixels), jnp.float32),
            pltpu.VMEM((pairs, tiles_y * strip, pixels), jnp.float32),
            pltpu.VMEM((pairs, tiles_y * strip, pixels), jnp.float32),
            pltpu.VMEM((tiles_y, strip, pixels), jnp.float32),
            pltpu.VMEM((tiles_y, strip, pixels), jnp.float32),
        ]
        + [pltpu.SemaphoreType.DMA((pairs,))] * 4
        + [pltpu.SemaphoreType.DMA((tiles_y,))] * 2,
        compiler_params=pltpu.CompilerParams(
            collective_id=1, has_side_effects=True, vmem_limit_bytes=48 * 1024 * 1024
        ),
    )(orders, shift, mask, weight, row_table, g_matrix)


def spectrum(extent, orders, period):
    wrapped = ((np.arange(orders) - orders // 2)[:, None] * np.arange(extent)[None, :]) % period
    angles = 2.0 * math.pi / period * wrapped
    return np.cos(angles).astype(np.float32), np.sin(angles).astype(np.float32)


def image_tables(pixels, orders_p, orders_q):
    cos_u, sin_u = spectrum(pixels, orders_p, pixels)
    row_table = np.concatenate((cos_u.T, sin_u.T), 1) * np.float32(1.0 / math.sqrt(orders_p))
    cos_v, sin_v = spectrum(pixels, orders_q, pixels)
    real_v = cos_v * np.float32(1.0 / math.sqrt(orders_q))
    imag_v = sin_v * np.float32(1.0 / math.sqrt(orders_q))
    g_matrix = np.block([[real_v, imag_v], [-imag_v, real_v]])
    return (row_table.astype(jnp.bfloat16), g_matrix.astype(jnp.bfloat16))


def body(
    fields, material_map, material_eps, material_loss, source_shift, source_mask, source_weight
):
    tiles_x = lax.axis_size("gx")
    tiles_y = lax.axis_size("gy")
    orders_p, orders_q = source_mask.shape[1:]
    final_fields, phasor = run_march(
        fields, material_map, material_eps, material_loss, tiles_x, tiles_y
    )
    period_x, period_y = phasor.shape[1:]
    cos_x, sin_x = spectrum(period_x, orders_p, period_x)
    cos_y, sin_y = spectrum(period_y, orders_q, period_y)
    both_y = jnp.asarray(np.concatenate((cos_y, sin_y), 0).T)
    along = jnp.dot(
        phasor.reshape(4 * period_x, period_y), both_y, precision=PRECISE
    ).reshape(2, 2, period_x, 2 * orders_q)
    part_re = along[0, :, :, :orders_q] + along[1, :, :, orders_q:]
    part_im = along[1, :, :, :orders_q] - along[0, :, :, orders_q:]
    both_x = jnp.asarray(np.concatenate((cos_x, sin_x), 1))
    stacked = jnp.concatenate(
        (
            jnp.concatenate((part_re, part_im), 2),
            jnp.concatenate((part_im, -part_re), 2),
        ),
        1,
    )
    orders = jnp.einsum("px,cxq->cpq", both_x, stacked, precision=PRECISE)
    scaling = 1.0 / math.sqrt(period_x * period_y * STEPS)
    orders_b = (orders * scaling).astype(jnp.bfloat16).reshape(2 * orders_p, 2 * orders_q)
    row_table, g_matrix = image_tables(M, orders_p, orders_q)
    image = run_picture(
        orders_b,
        source_shift,
        source_mask,
        source_weight,
        jnp.asarray(row_table),
        jnp.asarray(g_matrix),
        tiles_x,
        tiles_y,
    )
    return (final_fields, image)


def solution(mesh):
    placed = (
        P("clips", None, "gx", "gy"),
        P("clips", "gx", "gy"),
        P(),
        P(),
        P(("gx", "gy"), None),
        P(("gx", "gy"), None, None),
        P(("gx", "gy")),
    )
    return jax.shard_map(
        body,
        mesh=mesh,
        in_specs=placed,
        out_specs=(P("clips", None, "gx", "gy"), P(("gx", "gy"), "clips")),
        check_vma=False,
    )
```

```python
import functools
import math

import jax
import jax.numpy as jnp
import numpy as np
from jax import lax
from jax.experimental import pallas as pl
from jax.experimental.pallas import tpu as pltpu
from jax.sharding import PartitionSpec as P

STEPS = 12
M = 512
COURANT = 0.55
ANGULAR = 0.7
PRECISE = lax.Precision.HIGHEST
MESH = pl.DeviceIdType.MESH
GROUP = 32


def peer_at(index, tiles_y):
    return {"gx": index // tiles_y, "gy": lax.rem(index, tiles_y)}


def greet(me, count, tiles_y):
    barrier = pltpu.get_barrier_semaphore()

    def signal(k, unused):
        pl.semaphore_signal(
            barrier,
            inc=1,
            device_id=peer_at(lax.rem(me + k, count), tiles_y),
            device_id_type=MESH,
        )
        return unused

    lax.fori_loop(1, count, signal, 0)
    pl.semaphore_wait(barrier, count - 1)


def march(
    tiles_x,
    tiles_y,
    fields_ref,
    material_ref,
    eps_ref,
    loss_ref,
    final_ref,
    phasor_ref,
    e_ref,
    h_ref,
    keep_ref,
    curl_ref,
    row_out,
    row_e,
    row_h,
    col_out,
    col_e,
    col_h,
    row_g,
    col_g,
    row_d,
    col_d,
    row_far,
    col_far,
    phase,
    gathered,
    send_sem,
    recv_sem,
    gather_send,
    gather_recv,
    wave_ref,
):
    count = tiles_x * tiles_y
    depth, cells_x, cells_y = fields_ref.shape[1:]
    middle = depth // 2
    at_x = lax.axis_index("gx")
    at_y = lax.axis_index("gy")
    me = at_x * tiles_y + at_y
    tile = (cells_x, cells_y)
    row_id = lax.broadcasted_iota(jnp.int32, tile, 0)
    col_id = lax.broadcasted_iota(jnp.int32, tile, 1)
    last_row = row_id == cells_x - 1
    first_row = row_id == 0
    last_col = col_id == cells_y - 1
    first_col = col_id == 0
    blank = jnp.zeros(tile, jnp.float32)
    for turn in range(STEPS):
        moment = float(np.float32(ANGULAR) * np.float32(turn + 1))
        wave_ref[0, turn] = math.cos(moment)
        wave_ref[1, turn] = math.sin(moment)

    has_right_x = at_x < tiles_x - 1
    has_left_x = at_x > 0
    has_right_y = at_y < tiles_y - 1
    has_left_y = at_y > 0
    x_up, x_down = {"gx": at_x + 1}, {"gx": at_x - 1}
    y_up, y_down = {"gy": at_y + 1}, {"gy": at_y - 1}
    routes = (
        (row_out.at[0], row_e, x_down, has_left_x, has_right_x),
        (col_out.at[0], col_e, y_down, has_left_y, has_right_y),
        (row_far, row_g, x_up, has_right_x, has_left_x),
        (col_far, col_g, y_up, has_right_y, has_left_y),
        (
            row_far.at[2],
            row_d,
            {"gx": at_x + 1, "gy": at_y - 1},
            has_right_x & has_left_y,
            has_left_x & has_right_y,
        ),
        (
            col_far,
            col_d,
            {"gx": at_x - 1, "gy": at_y + 1},
            has_left_x & has_right_y,
            has_right_x & has_left_y,
        ),
        (row_out.at[1], row_h, x_up, has_right_x, has_left_x),
        (col_out.at[1], col_h, y_up, has_right_y, has_left_y),
    )

    def copy_of(slot, odd):
        source, target, device, _, _ = routes[slot]
        return pltpu.make_async_remote_copy(
            src_ref=source,
            dst_ref=target if slot > 5 else target.at[odd],
            send_sem=send_sem.at[slot],
            recv_sem=recv_sem.at[slot, odd],
            device_id=device,
            device_id_type=MESH,
        )

    def send(slot, odd):
        @pl.when(routes[slot][3])
        def _():
            copy_of(slot, odd).start()

    def sent(slot, odd):
        @pl.when(routes[slot][3])
        def _():
            copy_of(slot, odd).wait_send()

    def arrived(slot, odd):
        @pl.when(routes[slot][4])
        def _():
            copy_of(slot, odd).wait_recv()

    for halo in (row_e, row_h, col_e, col_h, row_g, col_g, row_d, col_d):
        halo[...] = jnp.zeros(halo.shape, jnp.float32)
    greet(me, count, tiles_y)

    keep_values = []
    curl_values = []
    for material in range(eps_ref.shape[0]):
        loss = jnp.full(tile, loss_ref[material], jnp.float32)
        eps = jnp.full(tile, eps_ref[material], jnp.float32)
        keep_values.append((1.0 - loss) / (1.0 + loss))
        curl_values.append(COURANT / (eps * (1.0 + loss)))
    for component in range(3):
        e_ref[component, depth] = blank
        h_ref[component, 0] = blank
    phase[...] = jnp.zeros(phase.shape, jnp.float32)

    def pack_columns(packed, z, first, second, column):
        packed = jnp.where(
            col_id == z, jnp.broadcast_to(first[:, column : column + 1], tile), packed
        )
        return jnp.where(
            col_id == depth + z,
            jnp.broadcast_to(second[:, column : column + 1], tile),
            packed,
        )

    def edges(z, ex, ey, ez, near, far):
        row_out[0, 0, pl.ds(z, 1), :] = ez[0:1]
        row_out[0, 1, pl.ds(z, 1), :] = ey[0:1]
        for place, values in enumerate((ez, ey, ex)):
            row_far[place, pl.ds(z, 1), :] = values[cells_x - 1 : cells_x]
        near = pack_columns(near, z, ez, ex, 0)
        far = pack_columns(far, z, ez, ex, cells_y - 1)
        far = jnp.where(
            col_id == 2 * depth + z,
            jnp.broadcast_to(ey[:, cells_y - 1 : cells_y], tile),
            far,
        )
        return near, far

    def load(block, packed):
        near, far, beyond = packed
        base = block * GROUP
        new = []
        for j in range(GROUP):
            materials = material_ref[base + j]
            keep = keep_values[0]
            curl = curl_values[0]
            for material in range(1, len(keep_values)):
                keep = jnp.where(materials == material, keep_values[material], keep)
                curl = jnp.where(materials == material, curl_values[material], curl)
            new.append((keep, curl, [fields_ref[c, base + j] for c in range(6)]))
        for j in range(GROUP):
            z = base + j
            keep_ref[z], curl_ref[z] = new[j][:2]
            values = new[j][2]
            for component in range(3):
                e_ref[component, z] = values[component]
                h_ref[component, z + 1] = values[3 + component]
            near, far = edges(z, values[0], values[1], values[2], near, far)
            row_out[1, 0, pl.ds(z, 1), :] = values[5][cells_x - 1 : cells_x]
            row_out[1, 1, pl.ds(z, 1), :] = values[4][cells_x - 1 : cells_x]
            beyond = pack_columns(beyond, z, values[5], values[3], cells_y - 1)
        return near, far, beyond

    col_out[0], col_far[...], col_out[1] = lax.fori_loop(
        0, depth // GROUP, load, (blank, blank, blank), unroll=True
    )
    for slot in range(8):
        send(slot, 0)
    for slot in (6, 7):
        arrived(slot, 0)

    plane = (depth, cells_y)
    depth_id = lax.broadcasted_iota(jnp.int32, plane, 0)
    plane_col = lax.broadcasted_iota(jnp.int32, plane, 1)
    keep_x = jnp.where(has_left_x, COURANT, 0.0)
    keep_y = jnp.where(has_left_y, COURANT, 0.0)

    def beyond_edges(odd):
        ez_g, ey_g, ex_g = row_g[odd, 0], row_g[odd, 1], row_g[odd, 2]
        ex_next = jnp.where(
            plane_col == cells_y - 1,
            pltpu.roll(row_d[odd], cells_y - 1, 1),
            pltpu.roll(ex_g, cells_y - 1, 1),
        )
        ex_up = jnp.where(depth_id == depth - 1, 0.0, pltpu.roll(ex_g, depth - 1, 0))
        row_h[0] = row_h[0] - keep_x * ((row_out[0, 1] - ey_g) - (ex_next - ex_g))
        row_h[1] = row_h[1] - keep_x * ((ex_up - ex_g) - (row_out[0, 0] - ez_g))

        near, far = col_out[0], col_g[odd]
        ahead = jnp.where(
            last_row, pltpu.roll(col_d[odd], cells_x - 1, 0), pltpu.roll(far, cells_x - 1, 0)
        )
        change = near - far
        dx_ey = pltpu.roll(ahead - far, cells_y - 2 * depth, 1)
        dy_ex = pltpu.roll(change, cells_y - depth, 1)
        up = jnp.where(col_id == 3 * depth - 1, 0.0, pltpu.roll(far, cells_y - 1, 1))
        dz_ey = pltpu.roll(up - far, cells_y - depth, 1)
        dy_ez = pltpu.roll(change, depth, 1)
        col_h[...] = col_h[...] - keep_y * jnp.where(
            col_id < depth, dx_ey - dy_ex, dy_ez - dz_ey
        )

    def step(turn, unused):
        odd = lax.rem(turn, 2)
        for slot in (0, 1):
            arrived(slot, odd)
        edge = col_e[odd]

        def magnetic(block, packed):
            base = block * GROUP
            ex = [e_ref[0, base + j] for j in range(GROUP + 1)]
            ey = [e_ref[1, base + j] for j in range(GROUP + 1)]
            ez = [e_ref[2, base + j] for j in range(GROUP)]
            new = []
            for j in range(GROUP):
                z = base + j
                row_z = jnp.broadcast_to(row_e[odd, 0, pl.ds(z, 1), :], tile)
                row_y = jnp.broadcast_to(row_e[odd, 1, pl.ds(z, 1), :], tile)
                col_z = pltpu.roll(edge, cells_y - 1 - z, 1)
                col_x = pltpu.roll(edge, cells_y - 1 - depth - z, 1)
                dx_ez = jnp.where(last_row, row_z, pltpu.roll(ez[j], cells_x - 1, 0)) - ez[j]
                dx_ey = jnp.where(last_row, row_y, pltpu.roll(ey[j], cells_x - 1, 0)) - ey[j]
                dy_ez = jnp.where(last_col, col_z, pltpu.roll(ez[j], cells_y - 1, 1)) - ez[j]
                dy_ex = jnp.where(last_col, col_x, pltpu.roll(ex[j], cells_y - 1, 1)) - ex[j]
                hx = h_ref[0, z + 1] - COURANT * (dy_ez - (ey[j + 1] - ey[j]))
                hy = h_ref[1, z + 1] - COURANT * ((ex[j + 1] - ex[j]) - dx_ez)
                hz = h_ref[2, z + 1] - COURANT * (dx_ey - dy_ex)
                new.append((hx, hy, hz))
            for j in range(GROUP):
                z = base + j
                hx, hy, hz = new[j]
                h_ref[0, z + 1] = hx
                h_ref[1, z + 1] = hy
                h_ref[2, z + 1] = hz
            return packed

        lax.fori_loop(0, depth // GROUP, magnetic, 0, unroll=True)
        for slot in (2, 3, 4, 5):
            arrived(slot, odd)
        beyond_edges(odd)
        for slot in range(6):
            sent(slot, odd)
        edge_h = col_h[...]

        def electric(block, packed):
            near, far = packed
            base = block * GROUP
            hx = [h_ref[0, base + j] for j in range(GROUP + 1)]
            hy = [h_ref[1, base + j] for j in range(GROUP + 1)]
            hz = [None] + [h_ref[2, base + j + 1] for j in range(GROUP)]
            new = []
            for j in range(1, GROUP + 1):
                z = base + j - 1
                row_z = jnp.broadcast_to(row_h[0, pl.ds(z, 1), :], tile)
                row_y = jnp.broadcast_to(row_h[1, pl.ds(z, 1), :], tile)
                col_z = pltpu.roll(edge_h, lax.rem(cells_y - z, cells_y), 1)
                col_x = pltpu.roll(edge_h, cells_y - depth - z, 1)
                dx_hz = hz[j] - jnp.where(first_row, row_z, pltpu.roll(hz[j], 1, 0))
                dx_hy = hy[j] - jnp.where(first_row, row_y, pltpu.roll(hy[j], 1, 0))
                dy_hz = hz[j] - jnp.where(first_col, col_z, pltpu.roll(hz[j], 1, 1))
                dy_hx = hx[j] - jnp.where(first_col, col_x, pltpu.roll(hx[j], 1, 1))
                keep, curl = keep_ref[z], curl_ref[z]
                ex = keep * e_ref[0, z] + curl * (dy_hz - (hy[j] - hy[j - 1]))
                ey = keep * e_ref[1, z] + curl * ((hx[j] - hx[j - 1]) - dx_hz)
                ez = keep * e_ref[2, z] + curl * (dx_hy - dy_hx)
                new.append((ex, ey, ez))
            for j in range(GROUP):
                z = base + j
                ex, ey, ez = new[j]
                e_ref[0, z] = ex
                e_ref[1, z] = ey
                e_ref[2, z] = ez
                near, far = edges(z, ex, ey, ez, near, far)
            return near, far

        col_out[0], col_far[...] = lax.fori_loop(
            0, depth // GROUP, electric, (blank, blank), unroll=True
        )

        @pl.when(turn < STEPS - 1)
        def _():
            for slot in (0, 1, 4, 5, 2, 3):
                send(slot, 1 - odd)

        for component in range(2):
            monitor = e_ref[component, middle]
            phase[component] = phase[component] + monitor * wave_ref[0, turn]
            phase[2 + component] = phase[2 + component] - monitor * wave_ref[1, turn]
        return unused

    lax.fori_loop(0, STEPS, step, 0)
    for slot in (6, 7):
        sent(slot, 0)

    def share(k):
        return pltpu.make_async_remote_copy(
            src_ref=phase,
            dst_ref=gathered.at[me],
            send_sem=gather_send.at[k],
            recv_sem=gather_recv.at[k],
            device_id=peer_at(lax.rem(me + k, count), tiles_y),
            device_id_type=MESH,
        )

    def start(k, unused):
        share(k).start()
        return unused

    lax.fori_loop(1, count, start, 0)

    def store(block, unused):
        base = block * GROUP
        values = [
            [e_ref[component, base + j] for component in range(3)]
            + [h_ref[component, base + j + 1] for component in range(3)]
            for j in range(GROUP)
        ]
        for j in range(GROUP):
            for component in range(6):
                final_ref[component, base + j] = values[j][component]
        return unused

    lax.fori_loop(0, depth // GROUP, store, 0, unroll=True)

    def finish(k, unused):
        share(k).wait_send()
        share(k).wait_recv()
        return unused

    lax.fori_loop(1, count, finish, 0)
    gathered[me] = phase[...]
    for tile_x in range(tiles_x):
        for tile_y in range(tiles_y):
            phasor_ref[
                :,
                tile_x * cells_x : (tile_x + 1) * cells_x,
                tile_y * cells_y : (tile_y + 1) * cells_y,
            ] = gathered[tile_x * tiles_y + tile_y]


def run_march(fields, material_map, material_eps, material_loss, tiles_x, tiles_y):
    depth, cells_x, cells_y = fields.shape[1:]
    count = tiles_x * tiles_y
    vmem = pl.BlockSpec(memory_space=pltpu.VMEM)
    smem = pl.BlockSpec(memory_space=pltpu.SMEM)
    state = (3, depth + 1, cells_x, cells_y)
    return pl.pallas_call(
        functools.partial(march, tiles_x, tiles_y),
        out_shape=(
            jax.ShapeDtypeStruct(fields.shape, jnp.float32),
            jax.ShapeDtypeStruct((4, cells_x * tiles_x, cells_y * tiles_y), jnp.float32),
        ),
        in_specs=[vmem, vmem, smem, smem],
        out_specs=(vmem, vmem),
        scratch_shapes=[
            pltpu.VMEM(state, jnp.float32),
            pltpu.VMEM(state, jnp.float32),
            pltpu.VMEM((depth, cells_x, cells_y), jnp.float32),
            pltpu.VMEM((depth, cells_x, cells_y), jnp.float32),
            pltpu.VMEM((2, 2, depth, cells_y), jnp.float32),
            pltpu.VMEM((2, 2, depth, cells_y), jnp.float32),
            pltpu.VMEM((2, depth, cells_y), jnp.float32),
            pltpu.VMEM((2, cells_x, cells_y), jnp.float32),
            pltpu.VMEM((2, cells_x, cells_y), jnp.float32),
            pltpu.VMEM((cells_x, cells_y), jnp.float32),
            pltpu.VMEM((2, 3, depth, cells_y), jnp.float32),
            pltpu.VMEM((2, cells_x, cells_y), jnp.float32),
            pltpu.VMEM((2, depth, cells_y), jnp.float32),
            pltpu.VMEM((2, cells_x, cells_y), jnp.float32),
            pltpu.VMEM((3, depth, cells_y), jnp.float32),
            pltpu.VMEM((cells_x, cells_y), jnp.float32),
            pltpu.VMEM((4, cells_x, cells_y), jnp.float32),
            pltpu.VMEM((count, 4, cells_x, cells_y), jnp.float32),
            pltpu.SemaphoreType.DMA((8,)),
            pltpu.SemaphoreType.DMA((8, 2)),
            pltpu.SemaphoreType.DMA((count,)),
            pltpu.SemaphoreType.DMA((count,)),
            pltpu.SMEM((2, STEPS), jnp.float32),
        ],
        compiler_params=pltpu.CompilerParams(
            collective_id=0, has_side_effects=True, vmem_limit_bytes=40 * 1024 * 1024
        ),
    )(fields, material_map, material_eps, material_loss)


def picture(
    tiles_x,
    tiles_y,
    orders_ref,
    shift_ref,
    mask_ref,
    weight_ref,
    rows_ref,
    g_ref,
    image_ref,
    columns,
    part,
    swapped,
    crossed,
    strips,
    landed,
    swap_send,
    swap_recv,
    cross_send,
    cross_recv,
    hand_send,
    hand_recv,
):
    count = tiles_x * tiles_y
    me = lax.axis_index("gx") * tiles_y + lax.axis_index("gy")
    sources = mask_ref.shape[0]
    size_p, size_q = mask_ref.shape[1:]
    pixels = image_ref.shape[1]
    strip = image_ref.shape[0]
    greet(me, count, tiles_y)

    def one_hot(size, offset, flipped):
        to_id = lax.broadcasted_iota(jnp.int32, (2 * size, 2 * size), 1 if flipped else 0)
        from_id = lax.broadcasted_iota(jnp.int32, (2 * size, 2 * size), 0 if flipped else 1)
        to_half = jnp.where(to_id >= size, size, 0)
        moved = to_id - to_half + offset
        moved = jnp.where(moved < 0, moved + size, moved)
        moved = jnp.where(moved >= size, moved - size, moved)
        return jnp.where(from_id == moved + to_half, 1.0, 0.0).astype(jnp.bfloat16)

    def prepare(source, unused):
        pick_p = one_hot(size_p, shift_ref[source, 0], False)
        pick_q = one_hot(size_q, shift_ref[source, 1], True)
        rolled = jnp.dot(pick_p, orders_ref[...], preferred_element_type=jnp.float32)
        rolled = jnp.dot(
            rolled.astype(jnp.bfloat16), pick_q, preferred_element_type=jnp.float32
        )
        passed = mask_ref[source].astype(jnp.float32)
        passed = jnp.concatenate((passed, passed), 1)
        passed = jnp.concatenate((passed, passed), 0)
        masked = (rolled * passed).astype(jnp.bfloat16)
        spread = jnp.dot(masked, g_ref[...], preferred_element_type=jnp.float32)
        spread = spread.astype(jnp.bfloat16)
        for block in range(2):
            real = spread[block * size_p : (block + 1) * size_p, :pixels]
            imag = spread[block * size_p : (block + 1) * size_p, pixels:]
            at = 2 * block * pixels
            columns[source, :size_p, at : at + pixels] = real
            columns[source, :size_p, at + pixels : at + 2 * pixels] = imag
            columns[source, size_p:, at : at + pixels] = -imag
            columns[source, size_p:, at + pixels : at + 2 * pixels] = real
        return unused

    lax.fori_loop(0, sources, prepare, 0, unroll=True)

    pairs = tiles_x // 2
    at_x = lax.axis_index("gx")
    at_y = lax.axis_index("gy")
    core = lax.rem(at_x, 2)
    at_pair = at_x // 2
    scale = 1.0 / (sources * count)
    high = tiles_y * strip

    def render(pair, half):
        table = rows_ref[
            pl.ds(pl.multiple_of((2 * pair + half) * high, high), high), :
        ]
        total = jnp.zeros((high, pixels), jnp.float32)
        for source in range(sources):
            bright = None
            for block in range(4):
                values = jnp.dot(
                    table,
                    columns[source, :, block * pixels : (block + 1) * pixels],
                    preferred_element_type=jnp.float32,
                )
                squared = values * values
                bright = squared if bright is None else bright + squared
            total = total + (weight_ref[source] * scale) * bright
        part[pair, half] = total

    def swap(pair):
        return pltpu.make_async_remote_copy(
            src_ref=part.at[pair, 1 - core],
            dst_ref=swapped.at[pair],
            send_sem=swap_send.at[pair],
            recv_sem=swap_recv.at[pair],
            device_id={"gx": at_x + 1 - 2 * core},
            device_id_type=MESH,
        )

    def cross(k):
        pair = lax.rem(at_pair + k, pairs)
        return pltpu.make_async_remote_copy(
            src_ref=part.at[pair, core],
            dst_ref=crossed.at[k],
            send_sem=cross_send.at[k],
            recv_sem=cross_recv.at[k],
            device_id={"gx": 2 * pair + core},
            device_id_type=MESH,
        )

    def away(k):
        return lax.rem(at_pair + k, pairs)

    def first(turn, unused):
        pair = away(turn + 1)
        render(pair, 1 - core)
        swap(pair).start()
        render(pair, core)
        return unused

    lax.fori_loop(0, pairs, first, 0)

    def second(turn, unused):
        pair = away(turn + 1)
        swap(pair).wait_recv()
        part[pair, core] = part[pair, core] + swapped[pair]

        @pl.when(turn < pairs - 1)
        def _():
            cross(turn + 1).start()

        return unused

    lax.fori_loop(0, pairs, second, 0)

    def gather_pairs(k, running):
        cross(k).wait_recv()
        return running + crossed[k]

    mine = lax.fori_loop(1, pairs, gather_pairs, part[at_pair, core])
    for owner in range(tiles_y):
        strips[owner] = mine[owner * strip : (owner + 1) * strip]

    def hand(k):
        owner = lax.rem(at_y + k, tiles_y)
        return pltpu.make_async_remote_copy(
            src_ref=strips.at[owner],
            dst_ref=landed.at[k],
            send_sem=hand_send.at[k],
            recv_sem=hand_recv.at[k],
            device_id={"gy": owner},
            device_id_type=MESH,
        )

    for k in range(1, tiles_y):
        hand(k).start()
    total = strips[at_y]
    for k in range(1, tiles_y):
        hand(k).wait_recv()
        total = total + landed[k]
    image_ref[...] = total
    for k in range(1, tiles_y):
        hand(k).wait_send()

    def finish(pair, unused):
        swap(pair).wait_send()

        @pl.when(pair > 0)
        def _():
            cross(pair).wait_send()

        return unused

    lax.fori_loop(0, pairs, finish, 0)


def run_picture(orders, shift, mask, weight, row_table, g_matrix, tiles_x, tiles_y):
    count = tiles_x * tiles_y
    pixels = row_table.shape[0]
    strip = pixels // count
    pairs = tiles_x // 2
    vmem = pl.BlockSpec(memory_space=pltpu.VMEM)
    smem = pl.BlockSpec(memory_space=pltpu.SMEM)
    return pl.pallas_call(
        functools.partial(picture, tiles_x, tiles_y),
        out_shape=jax.ShapeDtypeStruct((strip, pixels), jnp.float32),
        in_specs=[vmem, smem, vmem, smem, vmem, vmem],
        out_specs=vmem,
        scratch_shapes=[
            pltpu.VMEM((mask.shape[0], row_table.shape[1], 4 * pixels), jnp.bfloat16),
            pltpu.VMEM((pairs, 2, tiles_y * strip, pixels), jnp.float32),
            pltpu.VMEM((pairs, tiles_y * strip, pixels), jnp.float32),
            pltpu.VMEM((pairs, tiles_y * strip, pixels), jnp.float32),
            pltpu.VMEM((tiles_y, strip, pixels), jnp.float32),
            pltpu.VMEM((tiles_y, strip, pixels), jnp.float32),
        ]
        + [pltpu.SemaphoreType.DMA((pairs,))] * 4
        + [pltpu.SemaphoreType.DMA((tiles_y,))] * 2,
        compiler_params=pltpu.CompilerParams(
            collective_id=1, has_side_effects=True, vmem_limit_bytes=48 * 1024 * 1024
        ),
    )(orders, shift, mask, weight, row_table, g_matrix)


def spectrum(extent, orders, period):
    wrapped = ((np.arange(orders) - orders // 2)[:, None] * np.arange(extent)[None, :]) % period
    angles = 2.0 * math.pi / period * wrapped
    return np.cos(angles).astype(np.float32), np.sin(angles).astype(np.float32)


def image_tables(pixels, orders_p, orders_q):
    cos_u, sin_u = spectrum(pixels, orders_p, pixels)
    row_table = np.concatenate((cos_u.T, sin_u.T), 1) * np.float32(1.0 / math.sqrt(orders_p))
    cos_v, sin_v = spectrum(pixels, orders_q, pixels)
    real_v = cos_v * np.float32(1.0 / math.sqrt(orders_q))
    imag_v = sin_v * np.float32(1.0 / math.sqrt(orders_q))
    g_matrix = np.block([[real_v, imag_v], [-imag_v, real_v]])
    return (row_table.astype(jnp.bfloat16), g_matrix.astype(jnp.bfloat16))


def body(
    fields, material_map, material_eps, material_loss, source_shift, source_mask, source_weight
):
    tiles_x = lax.axis_size("gx")
    tiles_y = lax.axis_size("gy")
    orders_p, orders_q = source_mask.shape[1:]
    final_fields, phasor = run_march(
        fields, material_map, material_eps, material_loss, tiles_x, tiles_y
    )
    period_x, period_y = phasor.shape[1:]
    cos_x, sin_x = spectrum(period_x, orders_p, period_x)
    cos_y, sin_y = spectrum(period_y, orders_q, period_y)
    both_y = jnp.asarray(np.concatenate((cos_y, sin_y), 0).T)
    along = jnp.dot(
        phasor.reshape(4 * period_x, period_y), both_y, precision=PRECISE
    ).reshape(2, 2, period_x, 2 * orders_q)
    part_re = along[0, :, :, :orders_q] + along[1, :, :, orders_q:]
    part_im = along[1, :, :, :orders_q] - along[0, :, :, orders_q:]
    both_x = jnp.asarray(np.concatenate((cos_x, sin_x), 1))
    stacked = jnp.concatenate(
        (
            jnp.concatenate((part_re, part_im), 2),
            jnp.concatenate((part_im, -part_re), 2),
        ),
        1,
    )
    orders = jnp.einsum("px,cxq->cpq", both_x, stacked, precision=PRECISE)
    scaling = 1.0 / math.sqrt(period_x * period_y * STEPS)
    orders_b = (orders * scaling).astype(jnp.bfloat16).reshape(2 * orders_p, 2 * orders_q)
    row_table, g_matrix = image_tables(M, orders_p, orders_q)
    image = run_picture(
        orders_b,
        source_shift,
        source_mask,
        source_weight,
        jnp.asarray(row_table),
        jnp.asarray(g_matrix),
        tiles_x,
        tiles_y,
    )
    return (final_fields, image)


def solution(mesh):
    placed = (
        P("clips", None, "gx", "gy"),
        P("clips", "gx", "gy"),
        P(),
        P(),
        P(("gx", "gy"), None),
        P(("gx", "gy"), None, None),
        P(("gx", "gy")),
    )
    return jax.shard_map(
        body,
        mesh=mesh,
        in_specs=placed,
        out_specs=(P("clips", None, "gx", "gy"), P(("gx", "gy"), "clips")),
        check_vma=False,
    )
```
